128 devices in a mesh: cand: 16 (over y, z_hi, core), tp: 8 (over x, z_lo).
Axes of the slice: x: 4, y: 4, z: 4 (z_hi: 2, z_lo: 2; z = z_hi * 2 + z_lo), core: 2. Of those that a mesh axis runs over, the one named last changes fastest.
Arguments:
- tokens: bfloat16 [512, 24, 8192], P('cand', None, 'tp'), may hold values from -6 to 6
- norm_gain: bfloat16 [8192], replicated, may hold values from 0.5 to 1.5
- w_query: bfloat16 [8192, 4096], P(None, 'tp'), may hold values from -0.0625 to 0.0625
- b_query: bfloat16 [4096], P('tp'), may hold values from -5 to 5
- w_key: bfloat16 [8192, 1024], P(None, 'tp'), may hold values from -0.0625 to 0.0625
- b_key: bfloat16 [1024], P('tp'), may hold values from -5 to 5
- w_value: bfloat16 [8192, 1024], P(None, 'tp'), may hold values from -0.0625 to 0.0625
- b_value: bfloat16 [1024], P('tp'), may hold values from -5 to 5
- w_out: bfloat16 [4096, 8192], P('tp'), may hold values from -0.125 to 0.125
- prefix_keys: bfloat16 [32, 1024, 1024], P('cand', None, 'tp'), may hold values from -52 to 52
- prefix_values: bfloat16 [32, 1024, 1024], P('cand', None, 'tp'), may hold values from -6 to 6
- problem_slot: int32 [32], replicated, may hold values from 0 to 31, each once
- cand_problem: int32 [512, 1], P('cand'), may hold values from 0 to 31; in each aligned block of 32 rows (0 to 31, 32 to 63, ...) at most 2 rows name the same one
- step_len: int32 [512], P('cand'), may hold values from 1 to 24, as said below
Outputs:
- layer_out: bfloat16 [512, 24, 8192], P('cand', None, 'tp')
The draws below stay inside these ranges and needn't reach their ends.
Inputs may be any that keep to these rules, and one draw needn't show every extreme that they name: Problem p's prefix is stored at row problem_slot[p] of prefix_keys and prefix_values; every row belongs to exactly one problem. `cand_problem`: among the 32 candidates of one index of cand at most 2 belong to one problem; every problem has a candidate. `step_len`: step tokens at and after this length are padding; the lengths of the 32 candidates of one index of cand sum to at most 400, and to exactly 400 on the first index.
All inputs are finite; a program needn't handle non-finite values.
Results may differ from the reference program's by a relative error of at most 0.015.
Values may be sent and summed in bfloat16 or wider, within the bound.
No kernel may reach another device: no remote copies, remote signals or barrier semaphores. Data moves between devices by JAX's collectives and lax.ppermute only.
A program may use at most 192 MiB of HBM per device.

```python
import math
import jax
import jax.numpy as jnp
import numpy as np
from jax import lax

D = 8192
KV_HEADS = 8
HEAD = 128
QH = 32
PREFIX = 1024
STEP = 24
MOST = 2
CAND_DEV = 32
PROBLEMS = 32
CANDS = 512
N_TP = 8


def draw_prefix_keys(key, part):
    key = jax.random.fold_in(key, 11)
    full_shape = (PROBLEMS, PREFIX, KV_HEADS * HEAD)
    return jnp.clip(jax.random.normal(key, full_shape, jnp.float32), -6.0, 6.0).astype(jnp.bfloat16)


def draw_step_len(key, part):
    key = jax.random.fold_in(key, 23)
    blocks = CANDS // CAND_DEV
    pairs = CAND_DEV // 2
    first = jax.random.randint(jax.random.fold_in(key, 1), (blocks, pairs), 1, STEP + 1)
    first = first.at[:, 0].set(STEP)
    lowered = (jnp.arange(blocks) % 3)[:, None] * (jnp.arange(pairs)[None, :] == 1).astype(jnp.int32)
    second = jnp.maximum(STEP + 1 - first - lowered, 1)
    lengths = jnp.concatenate([first, second], 1)
    order = jax.vmap(lambda k: jax.random.permutation(k, CAND_DEV))(jax.random.split(jax.random.fold_in(key, 2), blocks))
    shuffled = jnp.take_along_axis(lengths, order, 1)
    return shuffled.reshape(CANDS).astype(jnp.int32)


def raised(entries, own_key, source, target, shards_of, factor):
    owner, partner = [(jnp.arange(entries.shape[dim]) // (entries.shape[dim] // shards_of)).reshape([-1 if axis == dim else 1 for axis in range(entries.ndim)]) for dim in (source, target)]
    chosen = jax.random.permutation(own_key, shards_of)[partner]
    strong = (owner == chosen) | (owner == (partner + shards_of // 2) % shards_of)
    return jnp.where(strong, factor * entries, entries)


def block_levels(stream_key, dims, shards, smallest, high):
    factor_of = 1.0
    for axis_at, shards_of in shards:
        draws = jax.random.uniform(jax.random.fold_in(jax.random.fold_in(stream_key, 6), axis_at), (shards_of,), jnp.float32, smallest / len(shards), high / len(shards))
        factor_of = factor_of * jnp.repeat(jnp.exp(draws), dims[axis_at] // shards_of).reshape((-1,) + (1,) * (len(dims) - 1 - axis_at))
    return factor_of


def assign_block(rng, own, number, rows, amount, top, reach, slope):
    order = jax.random.permutation(rng, amount)
    heavy_load, usual = load_shares(amount, rows * top, reach, slope, True), load_shares(amount, rows * top, reach, slope, False)
    places = jnp.arange(amount)

    def named(sizes, turn):
        used = int((sizes > 0).sum())
        fixed = max(1, used // 4)
        moved = fixed + (places - fixed + turn * (used - fixed)) % max(1, amount - fixed)
        return jnp.zeros((amount,), jnp.int32).at[order[jnp.where(places < fixed, places, moved)]].set(jnp.asarray(sizes, jnp.int32))

    sizes = jnp.where(number % 4 == 0, named(heavy_load, number // 4), named(usual, number - number // 4 - 1))
    mixed = jax.random.permutation(jax.random.fold_in(own, 3), amount)
    donor, sink = mixed[0:amount // 2 * 2:2], mixed[1:amount // 2 * 2:2]
    room = jnp.minimum(sizes[donor] - 1, reach - sizes[sink]) // 2
    room = jnp.where((donor == order[0]) | (sink == order[0]) | (sizes[sink] == 0), 0, jnp.maximum(room, 0))
    moved = jax.random.randint(jax.random.fold_in(own, 4), (amount // 2,), 0, 1 << 20) % (room + 1)
    sizes = sizes.at[donor].add(-moved).at[sink].add(moved)
    labels = jnp.searchsorted(jnp.cumsum(sizes), jnp.arange(rows * top), side="right").astype(jnp.int32)
    table = labels.reshape(top, rows).T
    table = table[jax.random.permutation(jax.random.fold_in(own, 1), rows)]
    turn = jax.random.randint(jax.random.fold_in(own, 2), (rows, 1), 0, top)
    return jnp.take_along_axis(table, (jnp.arange(top)[None, :] + turn) % top, axis=1)


def load_shares(amount, total, limit, skew, full):
    loads = [(1 << 20) // math.isqrt(grade ** skew) + 1 for grade in range(1, amount + 1)]
    largest = limit if full else min(limit, max(-(-total // amount), total * loads[0] // sum(loads)))
    least = 1 if total - largest >= amount - 1 else 0
    given, rest = [largest] + [least] * (amount - 1), total - largest - least * (amount - 1)
    while rest > 0:
        free = [i for i in range(1, amount) if given[i] < largest] or [i for i in range(1, amount) if given[i] < limit]
        mass, budget = sum([loads[i] for i in free]), rest
        for i in free:
            more = min(limit - given[i], max(1, budget * loads[i] // mass), rest)
            given[i] = given[i] + more
            rest = rest - more
    return np.array(given)


def normal_values(key, dims, width, most, cuts=(), kind=jnp.bfloat16):
    values = jax.random.normal(key, dims, jnp.float32) * width
    if len(cuts) > 0:
        values = block_levels(key, dims, cuts, -0.22, 0.18) * values
    return jnp.clip(values, min=-most, max=most).astype(kind)


def heavy_noise(rng, shape, deviation, reach, cuts, heavy, kind=jnp.bfloat16):
    values = deviation * jax.random.normal(rng, shape, jnp.float32)
    if cuts:
        values = values * block_levels(rng, shape, cuts, -0.22, 0.18)
    return jnp.clip(raised(values, jax.random.fold_in(rng, 3), *heavy), -reach, reach).astype(kind)


def setup_inputs(seed: int = 0) -> dict:
    arg_keys = jax.random.split(jax.random.key(seed), 15)
    tokens = normal_values(arg_keys[0], (CANDS, STEP, D), 1.0, 6.0, ((0, 16), (2, 8)))
    norm_gain = jnp.clip(1.0 + 0.1 * jax.random.normal(arg_keys[1], (D,), jnp.float32), 0.5, 1.5).astype(jnp.bfloat16)
    w_query = normal_values(arg_keys[2], (D, QH * HEAD), D ** -0.5, 0.0625, ((1, 8),))
    b_query = normal_values(arg_keys[3], (QH * HEAD,), 1.0, 5.0, ((0, 8),))
    w_key = normal_values(arg_keys[4], (D, KV_HEADS * HEAD), D ** -0.5, 0.0625, ((1, 8),))
    b_key = normal_values(arg_keys[5], (KV_HEADS * HEAD,), 1.0, 5.0, ((0, 8),))
    w_value = normal_values(arg_keys[6], (D, KV_HEADS * HEAD), D ** -0.5, 0.0625, ((1, 8),))
    b_value = normal_values(arg_keys[7], (KV_HEADS * HEAD,), 1.0, 5.0, ((0, 8),))
    w_out = heavy_noise(arg_keys[8], (QH * HEAD, D), (QH * HEAD) ** -0.5, 0.125, ((0, 8),), (0, 1, 8, 2.0))
    prefix_keys = draw_prefix_keys(jax.random.fold_in(arg_keys[14], 71), 0)
    prefix_values = normal_values(arg_keys[10], (PROBLEMS, PREFIX, KV_HEADS * HEAD), 1.0, 6.0, ((0, 16), (2, 8)))
    problem_slot = jax.random.permutation(arg_keys[11], PROBLEMS).astype(jnp.int32)
    cand_problem_keys = jax.random.split(jax.random.fold_in(arg_keys[12], 1), CANDS // CAND_DEV)
    cand_problem_turns = jax.random.permutation(jax.random.fold_in(arg_keys[12], 3), CANDS // CAND_DEV)
    cand_problem = jax.vmap(lambda own, number: assign_block(jax.random.fold_in(arg_keys[12], 2), own, number, CAND_DEV, PROBLEMS, 1, MOST, 2))(cand_problem_keys, cand_problem_turns).reshape((CANDS, 1))
    step_len = draw_step_len(jax.random.fold_in(arg_keys[14], 71), 0)
    return {"tokens": tokens, "norm_gain": norm_gain, "w_query": w_query, "b_query": b_query, "w_key": w_key, "b_key": b_key, "w_value": w_value, "b_value": b_value, "w_out": w_out, "prefix_keys": prefix_keys, "prefix_values": prefix_values, "problem_slot": problem_slot, "cand_problem": cand_problem, "step_len": step_len}


rope_base = 1000000.0
norm_eps = 1e-06

def rotary(inputs, offset):
    length = inputs.shape[1]
    half_size = inputs.shape[-1] // 2
    frequency = rope_base ** (-(jnp.arange(half_size, dtype=jnp.float32) * 2.0 / inputs.shape[-1]))
    angles = (offset + jnp.arange(length, dtype=jnp.float32))[:, None] * frequency[None, :]
    cosine = jnp.concatenate([jnp.cos(angles), jnp.cos(angles)], -1)[:, None, :]
    sine_table = jnp.concatenate([jnp.sin(angles), jnp.sin(angles)], -1)[:, None, :]
    turned = jnp.concatenate([-inputs[..., half_size:], inputs[..., :half_size]], -1)
    return inputs * cosine + turned * sine_table

def reference(tokens, norm_gain, w_query, b_query, w_key, b_key, w_value, b_value, w_out, prefix_keys, prefix_values, problem_slot, cand_problem, step_len):
    cand_count = tokens.shape[0]
    flat_rows = tokens.reshape(cand_count * STEP, D).astype(jnp.float32)
    normed = (flat_rows * lax.rsqrt(lax.optimization_barrier(jnp.mean(flat_rows * flat_rows, axis=-1, keepdims=True)) + norm_eps) * norm_gain.astype(jnp.float32)).astype(jnp.bfloat16)
    queries = jnp.dot(normed, w_query, preferred_element_type=jnp.float32) + b_query.astype(jnp.float32)
    new_keys = jnp.dot(normed, w_key, preferred_element_type=jnp.float32) + b_key.astype(jnp.float32)
    new_values = jnp.dot(normed, w_value, preferred_element_type=jnp.float32) + b_value.astype(jnp.float32)
    queries = rotary(queries.reshape(cand_count, STEP, QH, HEAD), PREFIX).astype(jnp.bfloat16)
    new_keys = rotary(new_keys.reshape(cand_count, STEP, KV_HEADS, HEAD), PREFIX).astype(jnp.bfloat16)
    new_values = new_values.astype(jnp.bfloat16).reshape(cand_count, STEP, KV_HEADS, HEAD)
    slot_rows = problem_slot[cand_problem[:, 0]].astype(jnp.int32)
    group_size = QH // KV_HEADS

    def attend(inputs):
        query_rows, key_rows, value_rows, slot_index, length = inputs
        old_keys = lax.dynamic_index_in_dim(prefix_keys, slot_index, 0, keepdims=False).reshape(PREFIX, KV_HEADS, HEAD)
        old_values = lax.dynamic_index_in_dim(prefix_values, slot_index, 0, keepdims=False).reshape(PREFIX, KV_HEADS, HEAD)
        all_keys = jnp.concatenate([old_keys, key_rows], 0).astype(jnp.float32)
        all_values = jnp.concatenate([old_values, value_rows], 0).astype(jnp.float32)
        grouped = query_rows.reshape(STEP, KV_HEADS, group_size, HEAD).astype(jnp.float32)
        scores = jnp.einsum('tkge,ske->tkgs', grouped, all_keys) * HEAD ** (-0.5)
        position = jnp.arange(PREFIX + STEP)
        query_pos = jnp.arange(STEP)
        allowed = (position[None, :] < PREFIX) | (position[None, :] - PREFIX <= query_pos[:, None]) & (position[None, :] - PREFIX < length)
        scores = jnp.where(allowed[:, None, None, :], scores, -1e+30)
        row_max = lax.optimization_barrier(jnp.max(scores, -1, keepdims=True))
        weights = jnp.exp(scores - row_max)
        row_sum = lax.optimization_barrier(jnp.sum(weights, -1))
        rounded = lax.optimization_barrier(weights.astype(jnp.bfloat16)).astype(jnp.float32)
        mixed_rows = jnp.einsum('tkgs,ske->tkge', rounded, all_values) / row_sum[..., None]
        return mixed_rows.astype(jnp.bfloat16).reshape(STEP, QH * HEAD)
    attended = lax.map(attend, (queries, new_keys, new_values, slot_rows, step_len))
    flat_att = attended.reshape(cand_count * STEP, QH * HEAD)
    width_part = QH * HEAD // N_TP
    summed = jnp.zeros((cand_count * STEP, D), jnp.float32)
    for member in range(N_TP):
        partial_term = jnp.dot(flat_att[:, member * width_part:(member + 1) * width_part], w_out[member * width_part:(member + 1) * width_part], preferred_element_type=jnp.float32)
        summed = summed + lax.optimization_barrier(partial_term.astype(jnp.bfloat16)).astype(jnp.float32)
    live_rows = (jnp.arange(STEP)[None, :] < step_len[:, None]).reshape(-1, 1)
    result = flat_rows + jnp.where(live_rows, summed, 0.0)
    return result.astype(jnp.bfloat16).reshape(cand_count, STEP, D)
```

```python
import functools

import jax
import jax.numpy as jnp
from jax import lax
from jax.experimental import pallas as pl
from jax.experimental.pallas import tpu as pltpu
from jax.sharding import PartitionSpec as P

HEAD = 128
LIVE = 400
CHUNKS = ((0, 400),)
PAD = 432
LOCAL = 16

rope_base = 1000000.0
norm_eps = 1e-06
bf16, f32 = jnp.bfloat16, jnp.float32


def along_x(d):
    return [(i, ((i // 2 + d) % 4) * 2 + i % 2) for i in range(8)]


def along_y(d):
    return [(i, ((i // 4 + d) % 4) * 4 + i % 4) for i in range(16)]


ACROSS_Z_LO = [(i, i ^ 1) for i in range(8)]
ACROSS_Z_HI = [(i, i ^ 2) for i in range(16)]
ACROSS_CORE = [(i, i ^ 1) for i in range(16)]


def dot(a, b):
    return jnp.dot(a, b, preferred_element_type=f32)


def gather_prefixes(prefix_keys, prefix_values):
    own = jnp.stack([prefix_keys, prefix_values], axis=1)
    low = lax.ppermute(own, "cand", along_y(1))
    high = lax.ppermute(own, "cand", along_y(-1))
    far0 = lax.ppermute(low[:1], "cand", along_y(1))
    far1 = lax.ppermute(high[1:], "cand", along_y(-1))
    mine = [own, high, far0, far1, low]
    return mine + [lax.ppermute(part, "cand", ACROSS_CORE) for part in mine]


def attention_kernel(bounds, n_rows, n_kv, meta, *refs):
    row_refs, kv_refs = refs[:n_rows], refs[n_rows : n_rows + n_kv]
    out_ref, kv_buf, rows, outs, sems = refs[n_rows + n_kv :]
    step = 24
    group = 4
    copies = []
    place = 0
    for i, ref in enumerate(kv_refs):
        count = ref.shape[0]
        copies.append(pltpu.make_async_copy(ref, kv_buf.at[pl.ds(place, count)], sems.at[i]))
        place += count
    for copy in copies:
        copy.start()
    at = 0
    for ref in row_refs:
        count = ref.shape[0]
        for i in range(group + 2):
            rows[i, at : at + count, :] = ref[:, i * HEAD : (i + 1) * HEAD].astype(f32)
        at += count
    for i in range(group + 2):
        rows[i, at:, :] = jnp.zeros((PAD - at, HEAD), f32)
    outs[...] = jnp.zeros_like(outs)
    for copy in copies:
        copy.wait()
    scale = HEAD ** (-0.5)
    t_at = lax.broadcasted_iota(jnp.int32, (group, step, step), 1).reshape(group * step, step)
    j_at = lax.broadcasted_iota(jnp.int32, (group * step, step), 1)

    def one(c, _):
        where, offset, length = meta[0, c], meta[1, c], meta[2, c]

        @pl.when(where >= 0)
        def _():
            here = pl.ds(offset, step)
            query = jnp.concatenate([rows[h, here, :] for h in range(group)], 0).astype(bf16)
            new_key = rows[group, here, :].astype(bf16)
            new_value = rows[group + 1, here, :].astype(bf16)
            contract = (((1,), (1,)), ((), ()))
            pre = lax.dot_general(query, kv_buf[where, 0], contract, preferred_element_type=f32) * scale
            own = lax.dot_general(query, new_key, contract, preferred_element_type=f32) * scale
            own = jnp.where((j_at <= t_at) & (j_at < length), own, -1e30)
            top = jnp.maximum(jnp.max(pre, -1, keepdims=True), jnp.max(own, -1, keepdims=True))
            pre = jnp.exp(pre - top)
            own = jnp.exp(own - top)
            total = jnp.sum(pre, -1, keepdims=True) + jnp.sum(own, -1, keepdims=True)
            mixed = dot(pre.astype(bf16), kv_buf[where, 1]) + dot(own.astype(bf16), new_value)
            mixed = mixed / total
            for h in range(group):
                outs[h, here, :] = mixed[h * step : (h + 1) * step]

        return 0

    lax.fori_loop(0, meta.shape[1], one, 0)
    first, last = bounds
    for h in range(group):
        out_ref[:, h * HEAD : (h + 1) * HEAD] = outs[h, first:last, :].astype(bf16)


def attention(bounds, meta, row_parts, kv_parts):
    first, last = bounds
    count = meta.shape[1]
    return pl.pallas_call(
        functools.partial(attention_kernel, bounds, len(row_parts), len(kv_parts)),
        out_shape=jax.ShapeDtypeStruct((last - first, 4 * HEAD), bf16),
        in_specs=[pl.BlockSpec(memory_space=pltpu.SMEM)]
        + [pl.BlockSpec(memory_space=pltpu.VMEM)] * len(row_parts)
        + [pl.BlockSpec(memory_space=pl.ANY)] * len(kv_parts),
        out_specs=pl.BlockSpec(memory_space=pltpu.VMEM),
        scratch_shapes=[
            pltpu.VMEM((LOCAL, 2, 1024, HEAD), bf16),
            pltpu.VMEM((6, PAD, HEAD), f32),
            pltpu.VMEM((4, PAD, HEAD), f32),
            pltpu.SemaphoreType.DMA((len(kv_parts),)),
        ],
        compiler_params=pltpu.CompilerParams(vmem_limit_bytes=40 * 2**20),
        cost_estimate=pl.CostEstimate(
            flops=2 * 2 * count * 96 * 1024 * HEAD,
            bytes_accessed=LOCAL * 2 * 1024 * HEAD * 2,
            transcendentals=count * 96 * 1024,
        ),
    )(meta, *row_parts, *kv_parts)


def on_device(
    tokens,
    norm_gain,
    w_query,
    b_query,
    w_key,
    b_key,
    w_value,
    b_value,
    w_out,
    prefix_keys,
    prefix_values,
    problem_slot,
    cand_problem,
    step_len,
):
    cand_count, step, width = tokens.shape
    tp_at, cand_at = lax.axis_index("tp"), lax.axis_index("cand")
    x_at, z_at = tp_at // 2, tp_at % 2
    y_at, half_at, core_at = cand_at // 4, (cand_at // 2) % 2, cand_at % 2

    problems = cand_problem[:, 0]
    slots = jnp.sum(
        jnp.where(
            problems[:, None] == jnp.arange(problem_slot.shape[0])[None, :],
            problem_slot[None, :],
            0,
        ),
        axis=1,
    )
    order = jnp.arange(cand_count)
    offsets = jnp.sum(jnp.where(order[None, :] < order[:, None], step_len[None, :], 0), axis=1)
    table = jnp.stack([slots, offsets, step_len])
    other_table = lax.ppermute(table, "cand", ACROSS_Z_HI)

    def local_place(slot):
        near = ((slot // 8 - y_at) % 4) * 2 + slot % 2 + 8 * (((slot // 2) % 2) ^ core_at)
        return jnp.where((slot // 4) % 2 == half_at, near, -1)

    def meta_of(table, bounds):
        slot, offset, length = table[0], table[1], table[2]
        inside = (offset < bounds[1]) & (offset + length > bounds[0])
        return jnp.stack([jnp.where(inside, local_place(slot), -1), offset, length])

    row_at = jnp.arange(LIVE)
    slot_row = (offsets[:, None] + jnp.arange(step)[None, :]).reshape(-1)
    alive = (jnp.arange(step)[None, :] < step_len[:, None]).reshape(-1)
    slot_row = jnp.where(alive, slot_row, -1)
    pick = (slot_row[None, :] == row_at[:, None]).astype(bf16)
    held = (row_at[:, None] >= offsets[None, :]) & (row_at[:, None] < (offsets + step_len)[None, :])
    position = jnp.sum(jnp.where(held, row_at[:, None] - offsets[None, :], 0), axis=1)
    is_near = jnp.any(held & (local_place(slots) >= 0)[None, :], axis=1)

    frequency = rope_base ** (-(jnp.arange(HEAD // 2, dtype=f32) * 2.0 / HEAD))
    angles = (prefix_keys.shape[1] + position.astype(f32))[:, None] * frequency[None, :]
    cosine = jnp.concatenate([jnp.cos(angles), jnp.cos(angles)], -1)
    sine = jnp.concatenate([-jnp.sin(angles), jnp.sin(angles)], -1)

    weights = jnp.concatenate([w_query, w_key, w_value], axis=1)
    bias = jnp.concatenate([b_query, b_key, b_value]).astype(f32)
    flat = tokens.reshape(cand_count * step, width)
    gain = norm_gain.astype(f32)

    kv_parts = gather_prefixes(prefix_keys, prefix_values)

    def project(bounds):
        first, last = bounds
        block = dot(pick[first:last], flat).astype(bf16)
        cut = width // 2
        across = lax.ppermute(block, "tp", ACROSS_Z_LO)
        blocks = []
        for part, z in ((block, z_at), (across, 1 - z_at)):
            low = lax.ppermute(part, "tp", along_x(1))
            high = lax.ppermute(part, "tp", along_x(-1))
            far0 = lax.ppermute(low[:, :cut], "tp", along_x(1))
            far1 = lax.ppermute(high[:, cut:], "tp", along_x(-1))
            far = ((x_at + 2) % 4) * 2 + z
            blocks += [
                (part, (x_at * 2 + z) * width),
                (low, (((x_at + 3) % 4) * 2 + z) * width),
                (high, (((x_at + 1) % 4) * 2 + z) * width),
                (far0, far * width),
                (far1, far * width + cut),
            ]
        total, squares = 0.0, 0.0
        for part, start in blocks:
            features = part.shape[1]
            wide = part.astype(f32)
            scaled = (wide * lax.dynamic_slice(gain, (start,), (features,))[None, :]).astype(bf16)
            total = total + dot(
                scaled, lax.dynamic_slice(weights, (start, 0), (features, weights.shape[1]))
            )
            squares = squares + jnp.sum(wide * wide, axis=1, keepdims=True)
        mean = squares / (8 * width)
        raw = total * lax.rsqrt(mean + norm_eps) + bias[None, :]
        cos_part, sin_part = cosine[first:last], sine[first:last]
        heads = []
        for h in range(5):
            head = raw[:, h * HEAD : (h + 1) * HEAD]
            heads.append(head * cos_part + jnp.roll(head, HEAD // 2, axis=1) * sin_part)
        heads.append(raw[:, 5 * HEAD :])
        return jnp.concatenate(heads, 1).astype(bf16)

    def scatter(attended):
        cut = width // 2

        def term(d, z):
            start = (((x_at + d) % 4) * 2 + z) * width
            return dot(attended, lax.dynamic_slice(w_out, (0, start), (w_out.shape[0], width)))

        sides = (1 - z_at, z_at)
        far = []
        for z in sides:
            block = term(2, z).astype(bf16)
            far.append(
                (
                    lax.ppermute(block[:, :cut], "tp", along_x(1)),
                    lax.ppermute(block[:, cut:], "tp", along_x(-1)),
                )
            )
        sums = []
        for z, (left, right) in zip(sides, far):
            up, down = term(1, z), term(3, z)
            up = jnp.concatenate([up[:, :cut] + left.astype(f32), up[:, cut:]], 1).astype(bf16)
            down = jnp.concatenate([down[:, :cut], down[:, cut:] + right.astype(f32)], 1).astype(bf16)
            up = lax.ppermute(up, "tp", along_x(1))
            down = lax.ppermute(down, "tp", along_x(-1))
            sums.append(term(0, z) + up.astype(f32) + down.astype(f32))
        return sums[1] + lax.ppermute(sums[0].astype(bf16), "tp", ACROSS_Z_LO).astype(f32)

    mine, theirs, updates = [], [], []
    for bounds in CHUNKS:
        part = project(bounds)
        mine.append(part)
        theirs.append(lax.ppermute(part, "cand", ACROSS_Z_HI))
        near = attention(bounds, meta_of(table, bounds), mine, kv_parts)
        for_other = attention(bounds, meta_of(other_table, bounds), theirs, kv_parts)
        back = lax.ppermute(for_other, "cand", ACROSS_Z_HI)
        attended = jnp.where(is_near[bounds[0] : bounds[1], None], near, back)
        updates.append(scatter(attended))
    update = jnp.concatenate(updates, 0)

    coarse = lax.reduce_precision(update, 8, 7)
    spread = (slot_row[:, None] == row_at[None, :]).astype(bf16)
    placed = dot(spread, coarse.astype(bf16)) + dot(spread, (update - coarse).astype(bf16))
    return (tokens.astype(f32) + placed.reshape(tokens.shape)).astype(bf16)


def solution(mesh):
    in_specs = (
        P("cand", None, "tp"),
        P(),
        P(None, "tp"),
        P("tp"),
        P(None, "tp"),
        P("tp"),
        P(None, "tp"),
        P("tp"),
        P("tp", None),
        P("cand", None, "tp"),
        P("cand", None, "tp"),
        P(),
        P("cand", None),
        P("cand"),
    )
    out_specs = P("cand", None, "tp")
    return jax.shard_map(
        on_device, mesh=mesh, in_specs=in_specs, out_specs=out_specs, check_vma=False
    )
```

```python
import functools

import jax
import jax.numpy as jnp
from jax import lax
from jax.experimental import pallas as pl
from jax.experimental.pallas import tpu as pltpu
from jax.sharding import PartitionSpec as P

HEAD = 128
LIVE = 400
ALL = (0, LIVE)
SIDE = 40
VMEM = 60 * 2**20
PAD = 432
LOCAL = 16

rope_base = 1000000.0
norm_eps = 1e-06
bf16, f32 = jnp.bfloat16, jnp.float32


def along_x(d):
    return [(i, ((i // 2 + d) % 4) * 2 + i % 2) for i in range(8)]


def along_y(d):
    return [(i, ((i // 4 + d) % 4) * 4 + i % 4) for i in range(16)]


ACROSS_Z_LO = [(i, i ^ 1) for i in range(8)]
ACROSS_Z_HI = [(i, i ^ 2) for i in range(16)]


def dot(a, b):
    return jnp.dot(a, b, preferred_element_type=f32)


SAME_HALF = [[i for i in range(16) if (i // 2) % 2 == half] for half in range(2)]


def gather_prefix(rows):
    every = lax.all_gather(rows, "cand", axis=0, axis_index_groups=SAME_HALF)
    return every.reshape((-1,) + rows.shape[1:])


def tie(values, *after):
    return lax.optimization_barrier((values, after))[0]


def finish_kernel(slot_row, tokens, term, up, down, crossed, out):
    update = term[...] + up[...].astype(f32) + down[...].astype(f32) + crossed[...].astype(f32)
    coarse = update.astype(bf16)
    fine = (update - coarse.astype(f32)).astype(bf16)
    at = lax.broadcasted_iota(jnp.int32, (tokens.shape[0], term.shape[0]), 1)
    spread = jnp.where(slot_row[...] == at, 1.0, 0.0).astype(bf16)
    placed = dot(spread, coarse) + dot(spread, fine)
    out[...] = (tokens[...].astype(f32) + placed).astype(bf16)


def finish(slot_row, tokens, *parts):
    tile = 256
    columns = lambda array: pl.BlockSpec((array.shape[0], tile), lambda i: (0, i))
    return pl.pallas_call(
        finish_kernel,
        out_shape=jax.ShapeDtypeStruct(tokens.shape, bf16),
        grid=(tokens.shape[1] // tile,),
        in_specs=[pl.BlockSpec((tokens.shape[0], 1), lambda i: (0, 0)), columns(tokens)]
        + [columns(part) for part in parts],
        out_specs=columns(tokens),
        compiler_params=pltpu.CompilerParams(vmem_limit_bytes=VMEM),
        cost_estimate=pl.CostEstimate(
            flops=4 * LIVE * tokens.size, bytes_accessed=8 * tokens.size, transcendentals=0
        ),
    )(slot_row[:, None], tokens, *parts)


def list_kernel(at, mine, other, problem_slot, out):
    half_at = at[0]
    for t, table in enumerate((mine, other)):

        def one(c, carry):
            offset, count0, count1 = carry
            slot, length = problem_slot[table[0, c]], table[1, c]
            place = (slot >> 3) * 4 + (slot & 3)
            side = place >> 3
            near = jnp.where(((slot >> 2) & 1) == half_at, 1, 0)
            to = jnp.where(side == 1, SIDE + count1, count0)
            out[t, 0, to] = place
            out[t, 1, to] = offset
            out[t, 2, to] = length
            return offset + length, count0 + near * (1 - side), count1 + near * side

        zero = jnp.int32(0)
        _, count0, count1 = lax.fori_loop(0, table.shape[1], one, (zero, zero, zero))
        for side, count in enumerate((count0, count1)):
            for r in range(3):
                out[t, r, side * SIDE + count] = out[t, r, side * SIDE]
            out[t, 3, side] = (count + 1) // 2


def candidate_lists(at, mine, other, problem_slot):
    return pl.pallas_call(
        list_kernel,
        out_shape=jax.ShapeDtypeStruct((2, 4, 2 * SIDE), jnp.int32),
        in_specs=[pl.BlockSpec(memory_space=pltpu.SMEM)] * 4,
        out_specs=pl.BlockSpec(memory_space=pltpu.SMEM),
    )(at, mine, other, problem_slot)


def attention_kernel(which, bounds, n_rows, n_kv, meta, *refs):
    row_refs, kv_refs = refs[:n_rows], refs[n_rows : n_rows + n_kv]
    out_ref, keys, values, rows, outs, sems = refs[n_rows + n_kv :]
    step = 24
    group = 4
    copies = []
    for side in range(2):
        held = pl.ds(side * LOCAL // 2, LOCAL // 2)
        for i, (ref, buffer) in enumerate(zip(kv_refs, (keys, values))):
            copies.append(pltpu.make_async_copy(ref.at[held], buffer.at[held], sems.at[2 * side + i]))
    for copy in copies:
        copy.start()
    at = 0
    for ref in row_refs:
        count = ref.shape[0]
        for i in range(group + 2):
            rows[i, at : at + count, :] = ref[:, i * HEAD : (i + 1) * HEAD].astype(f32)
        at += count
    for i in range(group + 2):
        rows[i, at:, :] = jnp.zeros((PAD - at, HEAD), f32)
    outs[...] = jnp.zeros_like(outs)
    scale = HEAD ** (-0.5)
    t_at = lax.broadcasted_iota(jnp.int32, (group, step, step), 1).reshape(group * step, step)
    j_at = lax.broadcasted_iota(jnp.int32, (group * step, step), 1)
    row_t = lax.broadcasted_iota(jnp.int32, (step, HEAD), 0)
    contract = (((1,), (1,)), ((), ()))

    def attend(where, offset, length):
        here = pl.ds(offset, step)
        query = jnp.concatenate([rows[h, here, :] for h in range(group)], 0).astype(bf16)
        new_key = rows[group, here, :].astype(bf16)
        new_value = rows[group + 1, here, :].astype(bf16)
        pre = lax.dot_general(query, keys[where], contract, preferred_element_type=f32)
        own = lax.dot_general(query, new_key, contract, preferred_element_type=f32)
        own = jnp.where((j_at <= t_at) & (j_at < length), own, -1e30)
        top = jnp.maximum(jnp.max(pre, -1, keepdims=True), jnp.max(own, -1, keepdims=True))
        pre = jnp.exp((pre - top) * scale)
        own = jnp.exp((own - top) * scale)
        total = jnp.sum(pre, -1, keepdims=True) + jnp.sum(own, -1, keepdims=True)
        mixed = dot(pre.astype(bf16), values[where]) + dot(own.astype(bf16), new_value)
        return mixed / total

    def two(first_at, i, _):
        entries = [[meta[which, r, first_at + 2 * i + j] for r in range(3)] for j in range(2)]
        results = [attend(*entry) for entry in entries]
        for (_, offset, length), mixed in zip(entries, results):
            here = pl.ds(offset, step)
            for h in range(group):
                new = mixed[h * step : (h + 1) * step]
                outs[h, here, :] = jnp.where(row_t < length, new, outs[h, here, :])
        return 0

    for side in range(2):
        for copy in copies[2 * side : 2 * side + 2]:
            copy.wait()
        lax.fori_loop(0, meta[which, 3, side], functools.partial(two, side * SIDE), 0)
    first, last = bounds
    for h in range(group):
        out_ref[:, h * HEAD : (h + 1) * HEAD] = outs[h, first:last, :].astype(bf16)


def attention(which, bounds, meta, row_parts, kv_parts):
    first, last = bounds
    count = 32
    return pl.pallas_call(
        functools.partial(attention_kernel, which, bounds, len(row_parts), len(kv_parts)),
        out_shape=jax.ShapeDtypeStruct((last - first, 4 * HEAD), bf16),
        in_specs=[pl.BlockSpec(memory_space=pltpu.SMEM)]
        + [pl.BlockSpec(memory_space=pltpu.VMEM)] * len(row_parts)
        + [pl.BlockSpec(memory_space=pl.ANY)] * len(kv_parts),
        out_specs=pl.BlockSpec(memory_space=pltpu.VMEM),
        scratch_shapes=[
            pltpu.VMEM((LOCAL, 1024, HEAD), bf16),
            pltpu.VMEM((LOCAL, 1024, HEAD), bf16),
            pltpu.VMEM((6, PAD, HEAD), f32),
            pltpu.VMEM((4, PAD, HEAD), f32),
            pltpu.SemaphoreType.DMA((4,)),
        ],
        compiler_params=pltpu.CompilerParams(vmem_limit_bytes=VMEM),
        cost_estimate=pl.CostEstimate(
            flops=2 * 2 * count * 96 * 1024 * HEAD,
            bytes_accessed=LOCAL * 2 * 1024 * HEAD * 2,
            transcendentals=count * 96 * 1024,
        ),
    )(meta, *row_parts, *kv_parts)


def on_device(
    tokens,
    norm_gain,
    w_query,
    b_query,
    w_key,
    b_key,
    w_value,
    b_value,
    w_out,
    prefix_keys,
    prefix_values,
    problem_slot,
    cand_problem,
    step_len,
):
    cand_count, step, width = tokens.shape
    tp_at, cand_at = lax.axis_index("tp"), lax.axis_index("cand")
    x_at, z_at = tp_at // 2, tp_at % 2
    half_at = (cand_at // 2) % 2

    z, o = z_at, 1 - z_at
    cut = width // 2

    def feature(d, z):
        return (((x_at + d) % 4) * 2 + z) * width

    def pass_up(part):
        return lax.ppermute(part, "tp", along_x(1))

    def pass_down(part):
        return lax.ppermute(part, "tp", along_x(-1))

    def pass_over(part):
        return lax.ppermute(part, "tp", ACROSS_Z_LO)

    problems = cand_problem[:, 0]
    order = jnp.arange(cand_count)
    offsets = jnp.sum(jnp.where(order[None, :] < order[:, None], step_len[None, :], 0), axis=1)
    row_at, step_at = jnp.arange(LIVE), jnp.arange(step)
    slot_row = jnp.where(
        step_at[None, :] < step_len[:, None], offsets[:, None] + step_at[None, :], -1
    ).reshape(-1)
    pick = (slot_row[None, :] == row_at[:, None]).astype(bf16)
    flat = tokens.reshape(cand_count * step, width)
    block = dot(pick, flat).astype(bf16)

    kv_parts = [gather_prefix(prefix_keys), gather_prefix(prefix_values)]

    low, high, across = pass_up(block), pass_down(block), pass_over(block)
    table = jnp.stack([problems, step_len])
    other_table = lax.ppermute(table, "cand", ACROSS_Z_HI)
    lists = candidate_lists(half_at[None], table, other_table, problem_slot)
    low, high, across = tie((low, high, across), lists)
    o_low, o_high = pass_up(across), pass_down(across)
    far0, far1 = pass_up(low[:, :cut]), pass_down(high[:, cut:])
    o_far0, o_far1 = pass_up(o_low[:, :cut]), pass_down(o_high[:, cut:])

    slots = jnp.sum(
        jnp.where(
            problems[:, None] == jnp.arange(problem_slot.shape[0])[None, :],
            problem_slot[None, :],
            0,
        ),
        axis=1,
    )
    is_near = ((slots // 4) % 2 == half_at).astype(bf16)
    traits = jnp.stack(
        [
            jnp.broadcast_to(step_at.astype(bf16)[None, :], (cand_count, step)),
            jnp.broadcast_to(is_near[:, None], (cand_count, step)),
        ],
        axis=-1,
    ).reshape(cand_count * step, 2)
    traits = dot(pick, traits)
    frequency = rope_base ** (-(jnp.arange(HEAD // 2, dtype=f32) * 2.0 / HEAD))
    angles = (prefix_keys.shape[1] + traits[:, :1]) * frequency[None, :]
    cosine = jnp.concatenate([jnp.cos(angles), jnp.cos(angles)], -1)
    sine = jnp.concatenate([-jnp.sin(angles), jnp.sin(angles)], -1)
    bias = jnp.concatenate([b_query, b_key, b_value]).astype(f32)[None, :]
    w_pair = jnp.concatenate([w_key, w_value], axis=1)
    gain = norm_gain.astype(f32)
    first = tie(block, low)
    blocks = [
        (first, feature(0, z)),
        (low, feature(3, z)),
        (high, feature(1, z)),
        (across, feature(0, o)),
        (far0, feature(2, z)),
        (far1, feature(2, z) + cut),
        (o_low, feature(3, o)),
        (o_high, feature(1, o)),
        (o_far0, feature(2, o)),
        (o_far1, feature(2, o) + cut),
    ]
    total, pair, squares = 0.0, 0.0, 0.0
    for part, start in blocks:
        features = part.shape[1]
        wide = part.astype(f32)
        scaled = (wide * lax.dynamic_slice(gain, (start,), (features,))[None, :]).astype(bf16)
        total = total + dot(
            scaled, lax.dynamic_slice(w_query, (start, 0), (features, w_query.shape[1]))
        )
        pair = pair + dot(
            scaled, lax.dynamic_slice(w_pair, (start, 0), (features, w_pair.shape[1]))
        )
        squares = squares + jnp.sum(wide * wide, axis=1, keepdims=True)
    scale = lax.rsqrt(squares / (8 * width) + norm_eps)
    raw = jnp.concatenate([total, pair], 1) * scale + bias
    heads = []
    for h in range(5):
        head = raw[:, h * HEAD : (h + 1) * HEAD]
        heads.append(head * cosine + jnp.roll(head, HEAD // 2, axis=1) * sine)
    heads.append(raw[:, 5 * HEAD :])
    rows = jnp.concatenate(heads, 1).astype(bf16)

    others = lax.ppermute(rows, "cand", ACROSS_Z_HI)
    near = attention(0, ALL, lists, [rows], kv_parts)
    others = tie(others, near)
    for_other = attention(1, ALL, lists, [others], kv_parts)
    back = lax.ppermute(for_other, "cand", ACROSS_Z_HI)
    attended = jnp.where(traits[:, 1:] > 0.5, near, back)

    def term(d, z, attended, first=0, last=width):
        start = feature(d, z) + first
        return dot(attended, lax.dynamic_slice(w_out, (0, start), (w_out.shape[0], last - first)))

    later, far = attended, []
    for side in (o, z):
        left = term(2, side, later, 0, cut).astype(bf16)
        right = term(2, side, tie(attended, left), cut, width).astype(bf16)
        far.append((pass_up(left), pass_down(right)))
        later = tie(attended, right)
    near_sums = []
    for side, (left, right) in zip((o, z), far):
        up, down = term(1, side, later), term(3, side, later)
        up = jnp.concatenate([up[:, :cut] + left.astype(f32), up[:, cut:]], 1).astype(bf16)
        down = jnp.concatenate([down[:, :cut], down[:, cut:] + right.astype(f32)], 1).astype(bf16)
        last = tie(attended, up, down)
        near_sums.append((term(0, side, last), pass_up(up), pass_down(down)))
    (own, up, down), rest = near_sums[0], near_sums[1]
    crossed = pass_over((own + up.astype(f32) + down.astype(f32)).astype(bf16))
    return finish(slot_row, flat, *rest, crossed).reshape(tokens.shape)


def solution(mesh):
    in_specs = (
        P("cand", None, "tp"),
        P(),
        P(None, "tp"),
        P("tp"),
        P(None, "tp"),
        P("tp"),
        P(None, "tp"),
        P("tp"),
        P("tp", None),
        P("cand", None, "tp"),
        P("cand", None, "tp"),
        P(),
        P("cand", None),
        P("cand"),
    )
    out_specs = P("cand", None, "tp")
    return jax.shard_map(
        on_device, mesh=mesh, in_specs=in_specs, out_specs=out_specs, check_vma=False
    )
```

```python
import functools

import jax
import jax.numpy as jnp
from jax import lax
from jax.experimental import pallas as pl
from jax.experimental.pallas import tpu as pltpu
from jax.sharding import PartitionSpec as P

HEAD = 128
LIVE = 400
ALL = (0, LIVE)
SIDE = 40
PAD = 432
LOCAL = 16

rope_base = 1000000.0
norm_eps = 1e-06
bf16, f32 = jnp.bfloat16, jnp.float32


def along_x(d):
    return [(i, ((i // 2 + d) % 4) * 2 + i % 2) for i in range(8)]


def along_y(d):
    return [(i, ((i // 4 + d) % 4) * 4 + i % 4) for i in range(16)]


ACROSS_Z_LO = [(i, i ^ 1) for i in range(8)]
ACROSS_Z_HI = [(i, i ^ 2) for i in range(16)]


def dot(a, b):
    return jnp.dot(a, b, preferred_element_type=f32)


ACROSS_CORE = [(i, i ^ 1) for i in range(16)]


def tie(values, *after):
    return lax.optimization_barrier((values, after))[0]


def project_kernel(n_parts, plan, has_sum, is_last, starts, *refs):
    parts, refs = refs[:n_parts], refs[n_parts:]
    gain, w_query, w_key, w_value = refs[:4]
    refs = refs[4:]
    if has_sum:
        sum_in, square_in = refs[:2]
        refs = refs[2:]
    if is_last:
        bias, cosine, sine, out, total, squares = refs
    else:
        sum_out, square_out, total, squares = refs
    at = pl.program_id(0)

    @pl.when(at == 0)
    def _():
        if has_sum:
            total[...] = sum_in[...]
            squares[...] = square_in[...]
        else:
            total[...] = jnp.zeros_like(total)
            squares[...] = jnp.zeros_like(squares)

    for place, pieces in enumerate(plan):

        @pl.when(at == place)
        def _(pieces=pieces):
            wide = [parts[i][first : first + count, :] for i, first, count in pieces]
            wide = jnp.concatenate(wide, 0).astype(f32)
            scaled = (wide * gain[...].astype(f32)).astype(bf16)
            total[:, :512] += dot(scaled, w_query[...])
            keys = jnp.concatenate([w_key[...], w_value[...]], 1)
            total[:, 512:] += dot(scaled, keys)
            square = wide * wide
            squares[...] += sum(square[:, i : i + HEAD] for i in range(0, square.shape[1], HEAD))

    @pl.when(at == len(plan) - 1)
    def _():
        if not is_last:
            sum_out[...] = total[...]
            square_out[...] = squares[...]
            return
        mean = jnp.sum(squares[...], axis=1, keepdims=True) / 8192.0
        raw = total[...] * lax.rsqrt(mean + norm_eps) + bias[...]
        for h in range(6):
            head = raw[:, h * HEAD : (h + 1) * HEAD]
            if h < 5:
                turned = jnp.concatenate([head[:, HEAD // 2 :], head[:, : HEAD // 2]], 1)
                head = head * cosine[...] + turned * sine[...]
            out[:, h * HEAD : (h + 1) * HEAD] = head.astype(bf16)


def project_parts(parts, plan, firsts, sums, last_args, gain, w_query, w_key, w_value):
    rows, deep = LIVE, parts[0].shape[1]
    starts = jnp.stack([first // deep for first in firsts])
    steps = starts.shape[0]
    whole = lambda array: pl.BlockSpec(array.shape, lambda i, s: (0,) * array.ndim)
    arrays = list(parts)
    operands = arrays + [gain, w_query, w_key, w_value]
    specs = [whole(array) for array in arrays] + [
        pl.BlockSpec((1, deep), lambda i, s: (0, s[i])),
        pl.BlockSpec((deep, w_query.shape[1]), lambda i, s: (s[i], 0)),
        pl.BlockSpec((deep, HEAD), lambda i, s: (s[i], 0)),
        pl.BlockSpec((deep, HEAD), lambda i, s: (s[i], 0)),
    ]
    if sums is not None:
        operands += list(sums)
        specs += [whole(array) for array in sums]
    if last_args is not None:
        operands += list(last_args)
        specs += [whole(array) for array in last_args]
        out_shape = jax.ShapeDtypeStruct((rows, 768), bf16)
        out_specs = pl.BlockSpec((rows, 768), lambda i, s: (0, 0))
    else:
        out_shape = (
            jax.ShapeDtypeStruct((rows, 768), f32),
            jax.ShapeDtypeStruct((rows, 128), f32),
        )
        out_specs = (
            pl.BlockSpec((rows, 768), lambda i, s: (0, 0)),
            pl.BlockSpec((rows, 128), lambda i, s: (0, 0)),
        )
    return pl.pallas_call(
        functools.partial(project_kernel, len(parts), plan, sums is not None, last_args is not None),
        out_shape=out_shape,
        grid_spec=pltpu.PrefetchScalarGridSpec(
            num_scalar_prefetch=1,
            grid=(steps,),
            in_specs=specs,
            out_specs=out_specs,
            scratch_shapes=[pltpu.VMEM((rows, 768), f32), pltpu.VMEM((rows, 128), f32)],
        ),
        compiler_params=pltpu.CompilerParams(vmem_limit_bytes=46 * 2**20),
        cost_estimate=pl.CostEstimate(
            flops=2 * rows * deep * steps * 768,
            bytes_accessed=steps * deep * 768 * 2,
            transcendentals=0,
        ),
    )(starts, *operands)


def finish_kernel(spread, tokens, term, up, down, crossed, out):
    update = term[...] + up[...].astype(f32) + down[...].astype(f32) + crossed[...].astype(f32)
    coarse = update.astype(bf16)
    fine = (update - coarse.astype(f32)).astype(bf16)
    placed = dot(spread[...], coarse) + dot(spread[...], fine)
    out[...] = (tokens[...].astype(f32) + placed).astype(bf16)


def finish(spread, tokens, *parts):
    tile = 256
    columns = lambda array: pl.BlockSpec((array.shape[0], tile), lambda i: (0, i))
    return pl.pallas_call(
        finish_kernel,
        out_shape=jax.ShapeDtypeStruct(tokens.shape, bf16),
        grid=(tokens.shape[1] // tile,),
        in_specs=[pl.BlockSpec(spread.shape, lambda i: (0, 0)), columns(tokens)]
        + [columns(part) for part in parts],
        out_specs=columns(tokens),
        compiler_params=pltpu.CompilerParams(vmem_limit_bytes=16 * 2**20),
        cost_estimate=pl.CostEstimate(
            flops=4 * LIVE * tokens.size, bytes_accessed=8 * tokens.size, transcendentals=0
        ),
    )(spread, tokens, *parts)


def list_kernel(at, mine, other, problem_slot, out):
    y_at, half_at, core_at = at[0], at[1], at[2]
    for t, table in enumerate((mine, other)):

        def one(c, carry):
            offset, count0, count1 = carry
            slot, length = problem_slot[table[0, c]], table[1, c]
            side = ((slot >> 1) & 1) ^ core_at
            place = ((y_at - (slot >> 3)) & 3) * 2 + (slot & 1) + 8 * side
            near = jnp.where(((slot >> 2) & 1) == half_at, 1, 0)
            to = jnp.where(side == 1, SIDE + count1, count0)
            out[t, 0, to] = place
            out[t, 1, to] = offset
            out[t, 2, to] = length
            return offset + length, count0 + near * (1 - side), count1 + near * side

        zero = jnp.int32(0)
        _, count0, count1 = lax.fori_loop(0, table.shape[1], one, (zero, zero, zero))
        for side, count in enumerate((count0, count1)):
            for r in range(3):
                out[t, r, side * SIDE + count] = out[t, r, side * SIDE]
            out[t, 3, side] = (count + 1) // 2


def candidate_lists(at, mine, other, problem_slot):
    return pl.pallas_call(
        list_kernel,
        out_shape=jax.ShapeDtypeStruct((2, 4, 2 * SIDE), jnp.int32),
        in_specs=[pl.BlockSpec(memory_space=pltpu.SMEM)] * 4,
        out_specs=pl.BlockSpec(memory_space=pltpu.SMEM),
    )(at, mine, other, problem_slot)


def attention_kernel(which, bounds, n_rows, n_kv, meta, *refs):
    row_refs, kv_refs = refs[:n_rows], refs[n_rows : n_rows + n_kv]
    out_ref, keys, values, rows, outs, sems = refs[n_rows + n_kv :]
    step = 24
    group = 4
    copies = []
    for side in range(2):
        for which_buffer, buffer in enumerate((keys, values)):
            for i in range(4):
                part = (which_buffer * 2 + side) * 4 + i
                behind = (4 - i) % 4 if which_buffer else i
                held = pl.ds(side * 8 + behind * 2, 2)
                copies.append(pltpu.make_async_copy(kv_refs[part], buffer.at[held], sems.at[part]))
    for copy in copies:
        copy.start()
    at = 0
    for ref in row_refs:
        count = ref.shape[0]
        for i in range(group + 2):
            rows[i, at : at + count, :] = ref[:, i * HEAD : (i + 1) * HEAD].astype(f32)
        at += count
    for i in range(group + 2):
        rows[i, at:, :] = jnp.zeros((PAD - at, HEAD), f32)
    outs[...] = jnp.zeros_like(outs)
    scale = HEAD ** (-0.5)
    t_at = lax.broadcasted_iota(jnp.int32, (group, step, step), 1).reshape(group * step, step)
    j_at = lax.broadcasted_iota(jnp.int32, (group * step, step), 1)
    row_t = lax.broadcasted_iota(jnp.int32, (step, HEAD), 0)
    contract = (((1,), (1,)), ((), ()))

    def attend(where, offset, length):
        here = pl.ds(offset, step)
        query = jnp.concatenate([rows[h, here, :] for h in range(group)], 0).astype(bf16)
        new_key = rows[group, here, :].astype(bf16)
        new_value = rows[group + 1, here, :].astype(bf16)
        pre = lax.dot_general(query, keys[where], contract, preferred_element_type=f32)
        own = lax.dot_general(query, new_key, contract, preferred_element_type=f32)
        own = jnp.where((j_at <= t_at) & (j_at < length), own, -1e30)
        top = jnp.maximum(jnp.max(pre, -1, keepdims=True), jnp.max(own, -1, keepdims=True))
        pre = jnp.exp((pre - top) * scale)
        own = jnp.exp((own - top) * scale)
        total = jnp.sum(pre, -1, keepdims=True) + jnp.sum(own, -1, keepdims=True)
        mixed = dot(pre.astype(bf16), values[where]) + dot(own.astype(bf16), new_value)
        return mixed / total

    def two(first_at, i, _):
        entries = [[meta[which, r, first_at + 2 * i + j] for r in range(3)] for j in range(2)]
        results = [attend(*entry) for entry in entries]
        for (_, offset, length), mixed in zip(entries, results):
            here = pl.ds(offset, step)
            for h in range(group):
                new = mixed[h * step : (h + 1) * step]
                outs[h, here, :] = jnp.where(row_t < length, new, outs[h, here, :])
        return 0

    for side in range(2):
        for copy in copies[8 * side : 8 * side + 8]:
            copy.wait()
        lax.fori_loop(0, meta[which, 3, side], functools.partial(two, side * SIDE), 0)
    first, last = bounds
    for h in range(group):
        out_ref[:, h * HEAD : (h + 1) * HEAD] = outs[h, first:last, :].astype(bf16)


def attention(which, bounds, meta, row_parts, kv_parts):
    first, last = bounds
    count = 32
    return pl.pallas_call(
        functools.partial(attention_kernel, which, bounds, len(row_parts), len(kv_parts)),
        out_shape=jax.ShapeDtypeStruct((last - first, 4 * HEAD), bf16),
        in_specs=[pl.BlockSpec(memory_space=pltpu.SMEM)]
        + [pl.BlockSpec(memory_space=pltpu.VMEM)] * len(row_parts)
        + [pl.BlockSpec(memory_space=pltpu.HBM)] * len(kv_parts),
        out_specs=pl.BlockSpec(memory_space=pltpu.VMEM),
        scratch_shapes=[
            pltpu.VMEM((LOCAL, 1024, HEAD), bf16),
            pltpu.VMEM((LOCAL, 1024, HEAD), bf16),
            pltpu.VMEM((6, PAD, HEAD), f32),
            pltpu.VMEM((4, PAD, HEAD), f32),
            pltpu.SemaphoreType.DMA((16,)),
        ],
        compiler_params=pltpu.CompilerParams(vmem_limit_bytes=28 * 2**20),
        cost_estimate=pl.CostEstimate(
            flops=2 * 2 * count * 96 * 1024 * HEAD,
            bytes_accessed=LOCAL * 2 * 1024 * HEAD * 2,
            transcendentals=count * 96 * 1024,
        ),
    )(meta, *row_parts, *kv_parts)


def on_device(
    tokens,
    norm_gain,
    w_query,
    b_query,
    w_key,
    b_key,
    w_value,
    b_value,
    w_out,
    prefix_keys,
    prefix_values,
    problem_slot,
    cand_problem,
    step_len,
):
    cand_count, step, width = tokens.shape
    tp_at, cand_at = lax.axis_index("tp"), lax.axis_index("cand")
    x_at, z_at = tp_at // 2, tp_at % 2
    y_at, half_at, core_at = cand_at // 4, (cand_at // 2) % 2, cand_at % 2

    z, o = z_at, 1 - z_at

    def feature(d, z):
        return (((x_at + d) % 4) * 2 + z) * width

    def pass_up(part):
        return lax.ppermute(part, "tp", along_x(1))

    def pass_down(part):
        return lax.ppermute(part, "tp", along_x(-1))

    def pass_over(part):
        return lax.ppermute(part, "tp", ACROSS_Z_LO)

    problems = cand_problem[:, 0]
    order = jnp.arange(cand_count)
    offsets = jnp.sum(jnp.where(order[None, :] < order[:, None], step_len[None, :], 0), axis=1)
    row_at, step_at = jnp.arange(LIVE), jnp.arange(step)
    slot_row = jnp.where(
        step_at[None, :] < step_len[:, None], offsets[:, None] + step_at[None, :], -1
    ).reshape(-1)
    pick = (slot_row[None, :] == row_at[:, None]).astype(bf16)
    spread = (slot_row[:, None] == row_at[None, :]).astype(bf16)
    flat = tokens.reshape(cand_count * step, width)
    block = dot(pick, flat).astype(bf16)

    low, high, across = pass_up(block), pass_down(block), pass_over(block)
    key_parts, value_parts = [prefix_keys], [prefix_values]

    def pass_prefixes():
        key_parts.append(lax.ppermute(key_parts[-1], "cand", along_y(1)))
        value_parts.append(lax.ppermute(value_parts[-1], "cand", along_y(-1)))

    pass_prefixes()
    table = jnp.stack([problems, step_len])
    low, high, across, key_parts[1], value_parts[1], late_table = tie(
        (low, high, across, key_parts[1], value_parts[1], table), block
    )
    o_low, o_high = pass_up(across), pass_down(across)
    other_table = lax.ppermute(late_table, "cand", ACROSS_Z_HI)
    pass_prefixes()
    lists = candidate_lists(
        jnp.stack([y_at, half_at, core_at]), table, other_table, problem_slot
    )
    add_up = functools.partial(
        project_parts, gain=norm_gain[None, :], w_query=w_query, w_key=w_key, w_value=w_value
    )
    all_rows = [((i, 0, LIVE),) for i in range(4)]
    sums = add_up(
        (block, low, high, across),
        all_rows,
        (feature(0, z), feature(3, z), feature(1, z), feature(0, o)),
        None,
        None,
    )
    o_low, o_high, low2, key_parts[2], value_parts[2], sums = tie(
        (o_low, o_high, low, key_parts[2], value_parts[2], sums), block
    )
    fars = pass_up(low2), pass_down(o_high)
    pass_prefixes()
    sums = add_up((o_low, o_high), all_rows[:2], (feature(3, o), feature(1, o)), sums, None)
    key_parts, value_parts, sums, lists = tie((key_parts, value_parts, sums, lists), block)
    kv_parts = [
        part
        for parts in (key_parts, value_parts)
        for part in parts + [lax.ppermute(part, "cand", ACROSS_CORE) for part in parts]
    ]

    slots = jnp.sum(
        jnp.where(
            problems[:, None] == jnp.arange(problem_slot.shape[0])[None, :],
            problem_slot[None, :],
            0,
        ),
        axis=1,
    )
    is_near = ((slots // 4) % 2 == half_at).astype(bf16)
    traits = jnp.stack(
        [
            jnp.broadcast_to(step_at.astype(bf16)[None, :], (cand_count, step)),
            jnp.broadcast_to(is_near[:, None], (cand_count, step)),
        ],
        axis=-1,
    ).reshape(cand_count * step, 2)
    traits = dot(pick, traits)
    frequency = rope_base ** (-(jnp.arange(HEAD // 2, dtype=f32) * 2.0 / HEAD))
    angles = (prefix_keys.shape[1] + traits[:, :1]) * frequency[None, :]
    cosine = jnp.concatenate([jnp.cos(angles), jnp.cos(angles)], -1)
    sine = jnp.concatenate([-jnp.sin(angles), jnp.sin(angles)], -1)
    bias = jnp.concatenate([b_query, b_key, b_value]).astype(f32)[None, :]
    last_args = bias, cosine, sine
    rows = add_up(fars, all_rows[:2], (feature(2, z), feature(2, o)), sums, last_args)

    others = lax.ppermute(rows, "cand", ACROSS_Z_HI)
    near = attention(0, ALL, lists, [rows], kv_parts)
    others = tie(others, near)
    for_other = attention(1, ALL, lists, [others], kv_parts)
    back = lax.ppermute(for_other, "cand", ACROSS_Z_HI)
    attended = jnp.where(traits[:, 1:] > 0.5, near, back)

    cut = width // 2

    def term(d, z, attended, first=0, last=width):
        start = feature(d, z) + first
        return dot(attended, lax.dynamic_slice(w_out, (0, start), (w_out.shape[0], last - first)))

    later, far = attended, []
    for side in (o, z):
        left = term(2, side, later, 0, cut).astype(bf16)
        right = term(2, side, tie(attended, left), cut, width).astype(bf16)
        far.append((pass_up(left), pass_down(right)))
        later = tie(attended, right)
    near_sums = []
    for side, (left, right) in zip((o, z), far):
        later = tie(attended, left, right)
        up, down = term(1, side, later), term(3, side, later)
        up = jnp.concatenate([up[:, :cut] + left.astype(f32), up[:, cut:]], 1).astype(bf16)
        down = jnp.concatenate([down[:, :cut], down[:, cut:] + right.astype(f32)], 1).astype(bf16)
        last = tie(attended, up, down)
        near_sums.append((term(0, side, last), pass_up(up), pass_down(down)))
    (own, up, down), rest = near_sums[0], near_sums[1]
    crossed = pass_over((own + up.astype(f32) + down.astype(f32)).astype(bf16))
    return finish(spread, flat, *rest, crossed).reshape(tokens.shape)


def solution(mesh):
    in_specs = (
        P("cand", None, "tp"),
        P(),
        P(None, "tp"),
        P("tp"),
        P(None, "tp"),
        P("tp"),
        P(None, "tp"),
        P("tp"),
        P("tp", None),
        P("cand", None, "tp"),
        P("cand", None, "tp"),
        P(),
        P("cand", None),
        P("cand"),
    )
    out_specs = P("cand", None, "tp")
    return jax.shard_map(
        on_device, mesh=mesh, in_specs=in_specs, out_specs=out_specs, check_vma=False
    )
```

```python
import functools

import jax
import jax.numpy as jnp
from jax import lax
from jax.experimental import pallas as pl
from jax.experimental.pallas import tpu as pltpu
from jax.sharding import PartitionSpec as P

HEAD = 128
LIVE = 400
ALL = (0, LIVE)
SIDE = 40
PAD = 432
LOCAL = 16

rope_base = 1000000.0
norm_eps = 1e-06
bf16, f32 = jnp.bfloat16, jnp.float32


def along_x(d):
    return [(i, ((i // 2 + d) % 4) * 2 + i % 2) for i in range(8)]


def along_y(d):
    return [(i, ((i // 4 + d) % 4) * 4 + i % 4) for i in range(16)]


ACROSS_Z_LO = [(i, i ^ 1) for i in range(8)]
ACROSS_Z_HI = [(i, i ^ 2) for i in range(16)]


def dot(a, b):
    return jnp.dot(a, b, preferred_element_type=f32)


ACROSS_CORE = [(i, i ^ 1) for i in range(16)]


def tie(values, *after):
    return lax.optimization_barrier((values, after))[0]


def project_kernel(n_parts, plan, has_sum, is_last, starts, *refs):
    parts, refs = refs[:n_parts], refs[n_parts:]
    gain, w_query, w_key, w_value = refs[:4]
    refs = refs[4:]
    if has_sum:
        sum_in, square_in = refs[:2]
        refs = refs[2:]
    if is_last:
        bias, cosine, sine, out, total, squares = refs
    else:
        sum_out, square_out, total, squares = refs
    at = pl.program_id(0)

    @pl.when(at == 0)
    def _():
        if has_sum:
            total[...] = sum_in[...]
            squares[...] = square_in[...]
        else:
            total[...] = jnp.zeros_like(total)
            squares[...] = jnp.zeros_like(squares)

    for place, pieces in enumerate(plan):

        @pl.when(at == place)
        def _(pieces=pieces):
            wide = [parts[i][first : first + count, :] for i, first, count in pieces]
            wide = jnp.concatenate(wide, 0).astype(f32)
            scaled = (wide * gain[...].astype(f32)).astype(bf16)
            total[:, :512] += dot(scaled, w_query[...])
            keys = jnp.concatenate([w_key[...], w_value[...]], 1)
            total[:, 512:] += dot(scaled, keys)
            square = wide * wide
            squares[...] += sum(square[:, i : i + HEAD] for i in range(0, square.shape[1], HEAD))

    @pl.when(at == len(plan) - 1)
    def _():
        if not is_last:
            sum_out[...] = total[...]
            square_out[...] = squares[...]
            return
        mean = jnp.sum(squares[...], axis=1, keepdims=True) / 8192.0
        raw = total[...] * lax.rsqrt(mean + norm_eps) + bias[...]
        for h in range(6):
            head = raw[:, h * HEAD : (h + 1) * HEAD]
            if h < 5:
                turned = jnp.concatenate([head[:, HEAD // 2 :], head[:, : HEAD // 2]], 1)
                head = head * cosine[...] + turned * sine[...]
            out[:, h * HEAD : (h + 1) * HEAD] = head.astype(bf16)


def project_parts(parts, plan, firsts, sums, last_args, gain, w_query, w_key, w_value):
    rows, deep = LIVE, parts[0].shape[1]
    starts = jnp.stack([first // deep for first in firsts])
    steps = starts.shape[0]
    whole = lambda array: pl.BlockSpec(array.shape, lambda i, s: (0,) * array.ndim)
    arrays = list(parts)
    operands = arrays + [gain, w_query, w_key, w_value]
    specs = [whole(array) for array in arrays] + [
        pl.BlockSpec((1, deep), lambda i, s: (0, s[i])),
        pl.BlockSpec((deep, w_query.shape[1]), lambda i, s: (s[i], 0)),
        pl.BlockSpec((deep, HEAD), lambda i, s: (s[i], 0)),
        pl.BlockSpec((deep, HEAD), lambda i, s: (s[i], 0)),
    ]
    if sums is not None:
        operands += list(sums)
        specs += [whole(array) for array in sums]
    if last_args is not None:
        operands += list(last_args)
        specs += [whole(array) for array in last_args]
        out_shape = jax.ShapeDtypeStruct((rows, 768), bf16)
        out_specs = pl.BlockSpec((rows, 768), lambda i, s: (0, 0))
    else:
        out_shape = (
            jax.ShapeDtypeStruct((rows, 768), f32),
            jax.ShapeDtypeStruct((rows, 128), f32),
        )
        out_specs = (
            pl.BlockSpec((rows, 768), lambda i, s: (0, 0)),
            pl.BlockSpec((rows, 128), lambda i, s: (0, 0)),
        )
    return pl.pallas_call(
        functools.partial(project_kernel, len(parts), plan, sums is not None, last_args is not None),
        out_shape=out_shape,
        grid_spec=pltpu.PrefetchScalarGridSpec(
            num_scalar_prefetch=1,
            grid=(steps,),
            in_specs=specs,
            out_specs=out_specs,
            scratch_shapes=[pltpu.VMEM((rows, 768), f32), pltpu.VMEM((rows, 128), f32)],
        ),
        compiler_params=pltpu.CompilerParams(vmem_limit_bytes=46 * 2**20),
        cost_estimate=pl.CostEstimate(
            flops=2 * rows * deep * steps * 768,
            bytes_accessed=steps * deep * 768 * 2,
            transcendentals=0,
        ),
    )(starts, *operands)


def finish_kernel(spread, tokens, term, up, down, crossed, out):
    update = term[...] + up[...].astype(f32) + down[...].astype(f32) + crossed[...].astype(f32)
    coarse = update.astype(bf16)
    fine = (update - coarse.astype(f32)).astype(bf16)
    placed = dot(spread[...], coarse) + dot(spread[...], fine)
    out[...] = (tokens[...].astype(f32) + placed).astype(bf16)


def finish(spread, tokens, *parts):
    tile = 256
    columns = lambda array: pl.BlockSpec((array.shape[0], tile), lambda i: (0, i))
    return pl.pallas_call(
        finish_kernel,
        out_shape=jax.ShapeDtypeStruct(tokens.shape, bf16),
        grid=(tokens.shape[1] // tile,),
        in_specs=[pl.BlockSpec(spread.shape, lambda i: (0, 0)), columns(tokens)]
        + [columns(part) for part in parts],
        out_specs=columns(tokens),
        compiler_params=pltpu.CompilerParams(vmem_limit_bytes=16 * 2**20),
        cost_estimate=pl.CostEstimate(
            flops=4 * LIVE * tokens.size, bytes_accessed=8 * tokens.size, transcendentals=0
        ),
    )(spread, tokens, *parts)


def list_kernel(at, mine, other, problem_slot, out):
    y_at, half_at, core_at = at[0], at[1], at[2]
    for t, table in enumerate((mine, other)):

        def one(c, carry):
            offset, count0, count1 = carry
            slot, length = problem_slot[table[0, c]], table[1, c]
            side = ((slot >> 1) & 1) ^ core_at
            place = ((y_at - (slot >> 3)) & 3) * 2 + (slot & 1) + 8 * side
            near = jnp.where(((slot >> 2) & 1) == half_at, 1, 0)
            to = jnp.where(side == 1, SIDE + count1, count0)
            out[t, 0, to] = place
            out[t, 1, to] = offset
            out[t, 2, to] = length
            return offset + length, count0 + near * (1 - side), count1 + near * side

        zero = jnp.int32(0)
        _, count0, count1 = lax.fori_loop(0, table.shape[1], one, (zero, zero, zero))
        for side, count in enumerate((count0, count1)):
            for r in range(3):
                out[t, r, side * SIDE + count] = out[t, r, side * SIDE]
            out[t, 3, side] = (count + 1) // 2


def candidate_lists(at, mine, other, problem_slot):
    return pl.pallas_call(
        list_kernel,
        out_shape=jax.ShapeDtypeStruct((2, 4, 2 * SIDE), jnp.int32),
        in_specs=[pl.BlockSpec(memory_space=pltpu.SMEM)] * 4,
        out_specs=pl.BlockSpec(memory_space=pltpu.SMEM),
    )(at, mine, other, problem_slot)


def attention_kernel(which, bounds, n_rows, n_kv, meta, *refs):
    row_refs, kv_refs = refs[:n_rows], refs[n_rows : n_rows + n_kv]
    out_ref, keys, values, rows, outs, sems = refs[n_rows + n_kv :]
    step = 24
    group = 4
    copies = []
    for side in range(2):
        for which_buffer, buffer in enumerate((keys, values)):
            for i in range(4):
                part = (which_buffer * 2 + side) * 4 + i
                behind = (4 - i) % 4 if which_buffer else i
                held = pl.ds(side * 8 + behind * 2, 2)
                copies.append(pltpu.make_async_copy(kv_refs[part], buffer.at[held], sems.at[part]))
    for copy in copies:
        copy.start()
    at = 0
    for ref in row_refs:
        count = ref.shape[0]
        for i in range(group + 2):
            rows[i, at : at + count, :] = ref[:, i * HEAD : (i + 1) * HEAD].astype(f32)
        at += count
    for i in range(group + 2):
        rows[i, at:, :] = jnp.zeros((PAD - at, HEAD), f32)
    outs[...] = jnp.zeros_like(outs)
    scale = HEAD ** (-0.5)
    t_at = lax.broadcasted_iota(jnp.int32, (group, step, step), 1).reshape(group * step, step)
    j_at = lax.broadcasted_iota(jnp.int32, (group * step, step), 1)
    row_t = lax.broadcasted_iota(jnp.int32, (step, HEAD), 0)
    contract = (((1,), (1,)), ((), ()))

    def attend(where, offset, length):
        here = pl.ds(offset, step)
        query = jnp.concatenate([rows[h, here, :] for h in range(group)], 0).astype(bf16)
        new_key = rows[group, here, :].astype(bf16)
        new_value = rows[group + 1, here, :].astype(bf16)
        pre = lax.dot_general(query, keys[where], contract, preferred_element_type=f32)
        own = lax.dot_general(query, new_key, contract, preferred_element_type=f32)
        own = jnp.where((j_at <= t_at) & (j_at < length), own, -1e30)
        top = jnp.maximum(jnp.max(pre, -1, keepdims=True), jnp.max(own, -1, keepdims=True))
        pre = jnp.exp((pre - top) * scale)
        own = jnp.exp((own - top) * scale)
        total = jnp.sum(pre, -1, keepdims=True) + jnp.sum(own, -1, keepdims=True)
        mixed = dot(pre.astype(bf16), values[where]) + dot(own.astype(bf16), new_value)
        return mixed / total

    def two(first_at, i, _):
        entries = [[meta[which, r, first_at + 2 * i + j] for r in range(3)] for j in range(2)]
        results = [attend(*entry) for entry in entries]
        for (_, offset, length), mixed in zip(entries, results):
            here = pl.ds(offset, step)
            for h in range(group):
                new = mixed[h * step : (h + 1) * step]
                outs[h, here, :] = jnp.where(row_t < length, new, outs[h, here, :])
        return 0

    for side in range(2):
        for copy in copies[8 * side : 8 * side + 8]:
            copy.wait()
        lax.fori_loop(0, meta[which, 3, side], functools.partial(two, side * SIDE), 0)
    first, last = bounds
    for h in range(group):
        out_ref[:, h * HEAD : (h + 1) * HEAD] = outs[h, first:last, :].astype(bf16)


def attention(which, bounds, meta, row_parts, kv_parts):
    first, last = bounds
    count = 32
    return pl.pallas_call(
        functools.partial(attention_kernel, which, bounds, len(row_parts), len(kv_parts)),
        out_shape=jax.ShapeDtypeStruct((last - first, 4 * HEAD), bf16),
        in_specs=[pl.BlockSpec(memory_space=pltpu.SMEM)]
        + [pl.BlockSpec(memory_space=pltpu.VMEM)] * len(row_parts)
        + [pl.BlockSpec(memory_space=pltpu.HBM)] * len(kv_parts),
        out_specs=pl.BlockSpec(memory_space=pltpu.VMEM),
        scratch_shapes=[
            pltpu.VMEM((LOCAL, 1024, HEAD), bf16),
            pltpu.VMEM((LOCAL, 1024, HEAD), bf16),
            pltpu.VMEM((6, PAD, HEAD), f32),
            pltpu.VMEM((4, PAD, HEAD), f32),
            pltpu.SemaphoreType.DMA((16,)),
        ],
        compiler_params=pltpu.CompilerParams(vmem_limit_bytes=28 * 2**20),
        cost_estimate=pl.CostEstimate(
            flops=2 * 2 * count * 96 * 1024 * HEAD,
            bytes_accessed=LOCAL * 2 * 1024 * HEAD * 2,
            transcendentals=count * 96 * 1024,
        ),
    )(meta, *row_parts, *kv_parts)


def on_device(
    tokens,
    norm_gain,
    w_query,
    b_query,
    w_key,
    b_key,
    w_value,
    b_value,
    w_out,
    prefix_keys,
    prefix_values,
    problem_slot,
    cand_problem,
    step_len,
):
    cand_count, step, width = tokens.shape
    tp_at, cand_at = lax.axis_index("tp"), lax.axis_index("cand")
    x_at, z_at = tp_at // 2, tp_at % 2
    y_at, half_at, core_at = cand_at // 4, (cand_at // 2) % 2, cand_at % 2

    z, o = z_at, 1 - z_at

    def feature(d, z):
        return (((x_at + d) % 4) * 2 + z) * width

    def pass_up(part):
        return lax.ppermute(part, "tp", along_x(1))

    def pass_down(part):
        return lax.ppermute(part, "tp", along_x(-1))

    def pass_over(part):
        return lax.ppermute(part, "tp", ACROSS_Z_LO)

    problems = cand_problem[:, 0]
    order = jnp.arange(cand_count)
    offsets = jnp.sum(jnp.where(order[None, :] < order[:, None], step_len[None, :], 0), axis=1)
    row_at, step_at = jnp.arange(LIVE), jnp.arange(step)
    slot_row = jnp.where(
        step_at[None, :] < step_len[:, None], offsets[:, None] + step_at[None, :], -1
    ).reshape(-1)
    pick = (slot_row[None, :] == row_at[:, None]).astype(bf16)
    spread = (slot_row[:, None] == row_at[None, :]).astype(bf16)
    flat = tokens.reshape(cand_count * step, width)
    block = dot(pick, flat).astype(bf16)

    low, high, across = pass_up(block), pass_down(block), pass_over(block)
    key_parts, value_parts = [prefix_keys], [prefix_values]

    def pass_prefixes():
        key_parts.append(lax.ppermute(key_parts[-1], "cand", along_y(1)))
        value_parts.append(lax.ppermute(value_parts[-1], "cand", along_y(-1)))

    pass_prefixes()
    table = jnp.stack([problems, step_len])
    low, high, across, key_parts[1], value_parts[1], late_table = tie(
        (low, high, across, key_parts[1], value_parts[1], table), block
    )
    o_low, o_high = pass_up(across), pass_down(across)
    other_table = lax.ppermute(late_table, "cand", ACROSS_Z_HI)
    pass_prefixes()
    add_up = functools.partial(
        project_parts, gain=norm_gain[None, :], w_query=w_query, w_key=w_key, w_value=w_value
    )
    all_rows = [((i, 0, LIVE),) for i in range(4)]
    sums = add_up(
        (block, low, high, across),
        all_rows,
        (feature(0, z), feature(3, z), feature(1, z), feature(0, o)),
        None,
        None,
    )
    o_low, o_high, low2, key_parts[2], value_parts[2], sums, other_table = tie(
        (o_low, o_high, low, key_parts[2], value_parts[2], sums, other_table), block
    )
    lists = candidate_lists(
        jnp.stack([y_at, half_at, core_at]), table, other_table, problem_slot
    )
    fars = pass_up(low2), pass_down(o_high)
    pass_prefixes()
    sums = add_up((o_low, o_high), all_rows[:2], (feature(3, o), feature(1, o)), sums, None)
    key_parts, value_parts, sums, lists = tie((key_parts, value_parts, sums, lists), block)
    kv_parts = [
        part
        for parts in (key_parts, value_parts)
        for part in parts + [lax.ppermute(part, "cand", ACROSS_CORE) for part in parts]
    ]

    slots = jnp.sum(
        jnp.where(
            problems[:, None] == jnp.arange(problem_slot.shape[0])[None, :],
            problem_slot[None, :],
            0,
        ),
        axis=1,
    )
    is_near = ((slots // 4) % 2 == half_at).astype(bf16)
    traits = jnp.stack(
        [
            jnp.broadcast_to(step_at.astype(bf16)[None, :], (cand_count, step)),
            jnp.broadcast_to(is_near[:, None], (cand_count, step)),
        ],
        axis=-1,
    ).reshape(cand_count * step, 2)
    traits = dot(pick, traits)
    frequency = rope_base ** (-(jnp.arange(HEAD // 2, dtype=f32) * 2.0 / HEAD))
    angles = (prefix_keys.shape[1] + traits[:, :1]) * frequency[None, :]
    cosine = jnp.concatenate([jnp.cos(angles), jnp.cos(angles)], -1)
    sine = jnp.concatenate([-jnp.sin(angles), jnp.sin(angles)], -1)
    bias = jnp.concatenate([b_query, b_key, b_value]).astype(f32)[None, :]
    last_args = bias, cosine, sine
    rows = add_up(fars, all_rows[:2], (feature(2, z), feature(2, o)), sums, last_args)

    others = lax.ppermute(rows, "cand", ACROSS_Z_HI)
    near = attention(0, ALL, lists, [rows], kv_parts)
    others = tie(others, near)
    for_other = attention(1, ALL, lists, [others], kv_parts)
    back = lax.ppermute(for_other, "cand", ACROSS_Z_HI)
    attended = jnp.where(traits[:, 1:] > 0.5, near, back)

    cut = width // 2

    def term(d, z, attended, first=0, last=width):
        start = feature(d, z) + first
        return dot(attended, lax.dynamic_slice(w_out, (0, start), (w_out.shape[0], last - first)))

    later, far = attended, []
    for side in (o, z):
        left = term(2, side, later, 0, cut).astype(bf16)
        right = term(2, side, tie(attended, left), cut, width).astype(bf16)
        far.append((pass_up(left), pass_down(right)))
        later = tie(attended, right)
    near_sums = []
    for side, (left, right) in zip((o, z), far):
        later = tie(attended, left, right)
        up, down = term(1, side, later), term(3, side, later)
        up = jnp.concatenate([up[:, :cut] + left.astype(f32), up[:, cut:]], 1).astype(bf16)
        down = jnp.concatenate([down[:, :cut], down[:, cut:] + right.astype(f32)], 1).astype(bf16)
        last = tie(attended, up, down)
        near_sums.append((term(0, side, last), pass_up(up), pass_down(down)))
    (own, up, down), rest = near_sums[0], near_sums[1]
    crossed = pass_over((own + up.astype(f32) + down.astype(f32)).astype(bf16))
    return finish(spread, flat, *rest, crossed).reshape(tokens.shape)


def solution(mesh):
    in_specs = (
        P("cand", None, "tp"),
        P(),
        P(None, "tp"),
        P("tp"),
        P(None, "tp"),
        P("tp"),
        P(None, "tp"),
        P("tp"),
        P("tp", None),
        P("cand", None, "tp"),
        P("cand", None, "tp"),
        P(),
        P("cand", None),
        P("cand"),
    )
    out_specs = P("cand", None, "tp")
    return jax.shard_map(
        on_device, mesh=mesh, in_specs=in_specs, out_specs=out_specs, check_vma=False
    )
```

```python
import functools

import jax
import jax.numpy as jnp
from jax import lax
from jax.experimental import pallas as pl
from jax.experimental.pallas import tpu as pltpu
from jax.sharding import PartitionSpec as P

HEAD = 128
LIVE = 400
ALL = (0, LIVE)
SIDE = 40
PAD = 432
LOCAL = 16

rope_base = 1000000.0
norm_eps = 1e-06
bf16, f32 = jnp.bfloat16, jnp.float32


def along_x(d):
    return [(i, ((i // 2 + d) % 4) * 2 + i % 2) for i in range(8)]


def along_y(d):
    return [(i, ((i // 4 + d) % 4) * 4 + i % 4) for i in range(16)]


ACROSS_Z_LO = [(i, i ^ 1) for i in range(8)]
ACROSS_Z_HI = [(i, i ^ 2) for i in range(16)]


def dot(a, b):
    return jnp.dot(a, b, preferred_element_type=f32)


ACROSS_CORE = [(i, i ^ 1) for i in range(16)]


def tie(values, *after):
    return lax.optimization_barrier((values, after))[0]


def project_kernel(n_parts, plan, has_sum, is_last, starts, *refs):
    parts, refs = refs[:n_parts], refs[n_parts:]
    gain, w_query, w_key, w_value = refs[:4]
    refs = refs[4:]
    if has_sum:
        sum_in, square_in = refs[:2]
        refs = refs[2:]
    if is_last:
        bias, cosine, sine, out, total, squares = refs
    else:
        sum_out, square_out, total, squares = refs
    at = pl.program_id(0)

    @pl.when(at == 0)
    def _():
        if has_sum:
            total[...] = sum_in[...]
            squares[...] = square_in[...]
        else:
            total[...] = jnp.zeros_like(total)
            squares[...] = jnp.zeros_like(squares)

    for place, pieces in enumerate(plan):

        @pl.when(at == place)
        def _(pieces=pieces):
            wide = [parts[i][first : first + count, :] for i, first, count in pieces]
            wide = jnp.concatenate(wide, 0).astype(f32)
            scaled = (wide * gain[...].astype(f32)).astype(bf16)
            total[:, :512] += dot(scaled, w_query[...])
            keys = jnp.concatenate([w_key[...], w_value[...]], 1)
            total[:, 512:] += dot(scaled, keys)
            square = wide * wide
            squares[...] += sum(square[:, i : i + HEAD] for i in range(0, square.shape[1], HEAD))

    @pl.when(at == len(plan) - 1)
    def _():
        if not is_last:
            sum_out[...] = total[...]
            square_out[...] = squares[...]
            return
        mean = jnp.sum(squares[...], axis=1, keepdims=True) / 8192.0
        raw = total[...] * lax.rsqrt(mean + norm_eps) + bias[...]
        for h in range(6):
            head = raw[:, h * HEAD : (h + 1) * HEAD]
            if h < 5:
                turned = jnp.concatenate([head[:, HEAD // 2 :], head[:, : HEAD // 2]], 1)
                head = head * cosine[...] + turned * sine[...]
            out[:, h * HEAD : (h + 1) * HEAD] = head.astype(bf16)


def project_parts(parts, plan, firsts, sums, last_args, gain, w_query, w_key, w_value):
    rows, deep = LIVE, parts[0].shape[1]
    starts = jnp.stack([first // deep for first in firsts])
    steps = starts.shape[0]
    whole = lambda array: pl.BlockSpec(array.shape, lambda i, s: (0,) * array.ndim)
    arrays = list(parts)
    operands = arrays + [gain, w_query, w_key, w_value]
    specs = [whole(array) for array in arrays] + [
        pl.BlockSpec((1, deep), lambda i, s: (0, s[i])),
        pl.BlockSpec((deep, w_query.shape[1]), lambda i, s: (s[i], 0)),
        pl.BlockSpec((deep, HEAD), lambda i, s: (s[i], 0)),
        pl.BlockSpec((deep, HEAD), lambda i, s: (s[i], 0)),
    ]
    if sums is not None:
        operands += list(sums)
        specs += [whole(array) for array in sums]
    if last_args is not None:
        operands += list(last_args)
        specs += [whole(array) for array in last_args]
        out_shape = jax.ShapeDtypeStruct((rows, 768), bf16)
        out_specs = pl.BlockSpec((rows, 768), lambda i, s: (0, 0))
    else:
        out_shape = (
            jax.ShapeDtypeStruct((rows, 768), f32),
            jax.ShapeDtypeStruct((rows, 128), f32),
        )
        out_specs = (
            pl.BlockSpec((rows, 768), lambda i, s: (0, 0)),
            pl.BlockSpec((rows, 128), lambda i, s: (0, 0)),
        )
    return pl.pallas_call(
        functools.partial(project_kernel, len(parts), plan, sums is not None, last_args is not None),
        out_shape=out_shape,
        grid_spec=pltpu.PrefetchScalarGridSpec(
            num_scalar_prefetch=1,
            grid=(steps,),
            in_specs=specs,
            out_specs=out_specs,
            scratch_shapes=[pltpu.VMEM((rows, 768), f32), pltpu.VMEM((rows, 128), f32)],
        ),
        compiler_params=pltpu.CompilerParams(vmem_limit_bytes=46 * 2**20),
        cost_estimate=pl.CostEstimate(
            flops=2 * rows * deep * steps * 768,
            bytes_accessed=steps * deep * 768 * 2,
            transcendentals=0,
        ),
    )(starts, *operands)


def finish_kernel(spread, tokens, term, up, down, crossed, out):
    update = term[...] + up[...].astype(f32) + down[...].astype(f32) + crossed[...].astype(f32)
    coarse = update.astype(bf16)
    fine = (update - coarse.astype(f32)).astype(bf16)
    placed = dot(spread[...], coarse) + dot(spread[...], fine)
    out[...] = (tokens[...].astype(f32) + placed).astype(bf16)


def finish(spread, tokens, *parts):
    tile = 256
    columns = lambda array: pl.BlockSpec((array.shape[0], tile), lambda i: (0, i))
    return pl.pallas_call(
        finish_kernel,
        out_shape=jax.ShapeDtypeStruct(tokens.shape, bf16),
        grid=(tokens.shape[1] // tile,),
        in_specs=[pl.BlockSpec(spread.shape, lambda i: (0, 0)), columns(tokens)]
        + [columns(part) for part in parts],
        out_specs=columns(tokens),
        compiler_params=pltpu.CompilerParams(vmem_limit_bytes=16 * 2**20),
        cost_estimate=pl.CostEstimate(
            flops=4 * LIVE * tokens.size, bytes_accessed=8 * tokens.size, transcendentals=0
        ),
    )(spread, tokens, *parts)


def list_kernel(at, mine, other, problem_slot, out):
    y_at, half_at, core_at = at[0], at[1], at[2]
    for t, table in enumerate((mine, other)):

        def one(c, carry):
            offset, count0, count1 = carry
            slot, length = problem_slot[table[0, c]], table[1, c]
            side = ((slot >> 1) & 1) ^ core_at
            place = ((y_at - (slot >> 3)) & 3) * 2 + (slot & 1) + 8 * side
            near = jnp.where(((slot >> 2) & 1) == half_at, 1, 0)
            to = jnp.where(side == 1, SIDE + count1, count0)
            out[t, 0, to] = place
            out[t, 1, to] = offset
            out[t, 2, to] = length
            return offset + length, count0 + near * (1 - side), count1 + near * side

        zero = jnp.int32(0)
        _, count0, count1 = lax.fori_loop(0, table.shape[1], one, (zero, zero, zero))
        for side, count in enumerate((count0, count1)):
            for r in range(3):
                out[t, r, side * SIDE + count] = out[t, r, side * SIDE]
            out[t, 3, side] = (count + 1) // 2


def candidate_lists(at, mine, other, problem_slot):
    return pl.pallas_call(
        list_kernel,
        out_shape=jax.ShapeDtypeStruct((2, 4, 2 * SIDE), jnp.int32),
        in_specs=[pl.BlockSpec(memory_space=pltpu.SMEM)] * 4,
        out_specs=pl.BlockSpec(memory_space=pltpu.SMEM),
    )(at, mine, other, problem_slot)


def attention_kernel(which, bounds, n_rows, n_kv, meta, *refs):
    row_refs, kv_refs = refs[:n_rows], refs[n_rows : n_rows + n_kv]
    out_ref, keys, values, rows, outs, sems = refs[n_rows + n_kv :]
    step = 24
    group = 4
    copies = []
    for side in range(2):
        for which_buffer, buffer in enumerate((keys, values)):
            for i in range(4):
                part = (which_buffer * 2 + side) * 4 + i
                behind = (4 - i) % 4 if which_buffer else i
                held = pl.ds(side * 8 + behind * 2, 2)
                copies.append(pltpu.make_async_copy(kv_refs[part], buffer.at[held], sems.at[part]))
    for copy in copies:
        copy.start()
    at = 0
    for ref in row_refs:
        count = ref.shape[0]
        for i in range(group + 2):
            rows[i, at : at + count, :] = ref[:, i * HEAD : (i + 1) * HEAD].astype(f32)
        at += count
    for i in range(group + 2):
        rows[i, at:, :] = jnp.zeros((PAD - at, HEAD), f32)
    outs[...] = jnp.zeros_like(outs)
    scale = HEAD ** (-0.5)
    t_at = lax.broadcasted_iota(jnp.int32, (group, step, step), 1).reshape(group * step, step)
    j_at = lax.broadcasted_iota(jnp.int32, (group * step, step), 1)
    row_t = lax.broadcasted_iota(jnp.int32, (step, HEAD), 0)
    contract = (((1,), (1,)), ((), ()))

    def attend(where, offset, length):
        here = pl.ds(offset, step)
        query = jnp.concatenate([rows[h, here, :] for h in range(group)], 0).astype(bf16)
        new_key = rows[group, here, :].astype(bf16)
        new_value = rows[group + 1, here, :].astype(bf16)
        pre = lax.dot_general(query, keys[where], contract, preferred_element_type=f32)
        own = lax.dot_general(query, new_key, contract, preferred_element_type=f32)
        own = jnp.where((j_at <= t_at) & (j_at < length), own, -1e30)
        top = jnp.maximum(jnp.max(pre, -1, keepdims=True), jnp.max(own, -1, keepdims=True))
        pre = jnp.exp((pre - top) * scale)
        own = jnp.exp((own - top) * scale)
        total = jnp.sum(pre, -1, keepdims=True) + jnp.sum(own, -1, keepdims=True)
        mixed = dot(pre.astype(bf16), values[where]) + dot(own.astype(bf16), new_value)
        return mixed / total

    def two(first_at, i, _):
        entries = [[meta[which, r, first_at + 2 * i + j] for r in range(3)] for j in range(2)]
        results = [attend(*entry) for entry in entries]
        for (_, offset, length), mixed in zip(entries, results):
            here = pl.ds(offset, step)
            for h in range(group):
                new = mixed[h * step : (h + 1) * step]
                outs[h, here, :] = jnp.where(row_t < length, new, outs[h, here, :])
        return 0

    for side in range(2):
        for copy in copies[8 * side : 8 * side + 8]:
            copy.wait()
        lax.fori_loop(0, meta[which, 3, side], functools.partial(two, side * SIDE), 0)
    first, last = bounds
    for h in range(group):
        out_ref[:, h * HEAD : (h + 1) * HEAD] = outs[h, first:last, :].astype(bf16)


def attention(which, bounds, meta, row_parts, kv_parts):
    first, last = bounds
    count = 32
    return pl.pallas_call(
        functools.partial(attention_kernel, which, bounds, len(row_parts), len(kv_parts)),
        out_shape=jax.ShapeDtypeStruct((last - first, 4 * HEAD), bf16),
        in_specs=[pl.BlockSpec(memory_space=pltpu.SMEM)]
        + [pl.BlockSpec(memory_space=pltpu.VMEM)] * len(row_parts)
        + [pl.BlockSpec(memory_space=pltpu.HBM)] * len(kv_parts),
        out_specs=pl.BlockSpec(memory_space=pltpu.VMEM),
        scratch_shapes=[
            pltpu.VMEM((LOCAL, 1024, HEAD), bf16),
            pltpu.VMEM((LOCAL, 1024, HEAD), bf16),
            pltpu.VMEM((6, PAD, HEAD), f32),
            pltpu.VMEM((4, PAD, HEAD), f32),
            pltpu.SemaphoreType.DMA((16,)),
        ],
        compiler_params=pltpu.CompilerParams(vmem_limit_bytes=28 * 2**20),
        cost_estimate=pl.CostEstimate(
            flops=2 * 2 * count * 96 * 1024 * HEAD,
            bytes_accessed=LOCAL * 2 * 1024 * HEAD * 2,
            transcendentals=count * 96 * 1024,
        ),
    )(meta, *row_parts, *kv_parts)


def on_device(
    tokens,
    norm_gain,
    w_query,
    b_query,
    w_key,
    b_key,
    w_value,
    b_value,
    w_out,
    prefix_keys,
    prefix_values,
    problem_slot,
    cand_problem,
    step_len,
):
    cand_count, step, width = tokens.shape
    tp_at, cand_at = lax.axis_index("tp"), lax.axis_index("cand")
    x_at, z_at = tp_at // 2, tp_at % 2
    y_at, half_at, core_at = cand_at // 4, (cand_at // 2) % 2, cand_at % 2

    z, o = z_at, 1 - z_at

    def feature(d, z):
        return (((x_at + d) % 4) * 2 + z) * width

    def pass_up(part):
        return lax.ppermute(part, "tp", along_x(1))

    def pass_down(part):
        return lax.ppermute(part, "tp", along_x(-1))

    def pass_over(part):
        return lax.ppermute(part, "tp", ACROSS_Z_LO)

    problems = cand_problem[:, 0]
    order = jnp.arange(cand_count)
    offsets = jnp.sum(jnp.where(order[None, :] < order[:, None], step_len[None, :], 0), axis=1)
    row_at, step_at = jnp.arange(LIVE), jnp.arange(step)
    slot_row = jnp.where(
        step_at[None, :] < step_len[:, None], offsets[:, None] + step_at[None, :], -1
    ).reshape(-1)
    pick = (slot_row[None, :] == row_at[:, None]).astype(bf16)
    spread = (slot_row[:, None] == row_at[None, :]).astype(bf16)
    flat = tokens.reshape(cand_count * step, width)
    block = dot(pick, flat).astype(bf16)

    low, high, across = pass_up(block), pass_down(block), pass_over(block)
    key_parts, value_parts = [prefix_keys], [prefix_values]

    def pass_prefixes():
        key_parts.append(lax.ppermute(key_parts[-1], "cand", along_y(1)))
        value_parts.append(lax.ppermute(value_parts[-1], "cand", along_y(-1)))

    pass_prefixes()
    table = jnp.stack([problems, step_len])
    low, high, across, key_parts[1], value_parts[1], late_table = tie(
        (low, high, across, key_parts[1], value_parts[1], table), block
    )
    o_low, o_high = pass_up(across), pass_down(across)
    other_table = lax.ppermute(late_table, "cand", ACROSS_Z_HI)
    pass_prefixes()
    add_up = functools.partial(
        project_parts, gain=norm_gain[None, :], w_query=w_query, w_key=w_key, w_value=w_value
    )
    all_rows = [((i, 0, LIVE),) for i in range(4)]
    sums = add_up(
        (block, low, high, across),
        all_rows,
        (feature(0, z), feature(3, z), feature(1, z), feature(0, o)),
        None,
        None,
    )
    o_low, o_high, low2, key_parts[2], value_parts[2], sums, other_table = tie(
        (o_low, o_high, low, key_parts[2], value_parts[2], sums, other_table), block
    )
    lists = candidate_lists(
        jnp.stack([y_at, half_at, core_at]), table, other_table, problem_slot
    )
    fars = pass_up(low2), pass_down(o_high)
    pass_prefixes()
    sums = add_up((o_low, o_high), all_rows[:2], (feature(3, o), feature(1, o)), sums, None)
    key_parts, value_parts, sums, lists = tie((key_parts, value_parts, sums, lists), block)
    kv_parts = [
        part
        for parts in (key_parts, value_parts)
        for part in parts + [lax.ppermute(part, "cand", ACROSS_CORE) for part in parts]
    ]

    slots = jnp.sum(
        jnp.where(
            problems[:, None] == jnp.arange(problem_slot.shape[0])[None, :],
            problem_slot[None, :],
            0,
        ),
        axis=1,
    )
    is_near = ((slots // 4) % 2 == half_at).astype(bf16)
    traits = jnp.stack(
        [
            jnp.broadcast_to(step_at.astype(bf16)[None, :], (cand_count, step)),
            jnp.broadcast_to(is_near[:, None], (cand_count, step)),
        ],
        axis=-1,
    ).reshape(cand_count * step, 2)
    traits = dot(pick, traits)
    frequency = rope_base ** (-(jnp.arange(HEAD // 2, dtype=f32) * 2.0 / HEAD))
    angles = (prefix_keys.shape[1] + traits[:, :1]) * frequency[None, :]
    cosine = jnp.concatenate([jnp.cos(angles), jnp.cos(angles)], -1)
    sine = jnp.concatenate([-jnp.sin(angles), jnp.sin(angles)], -1)
    bias = jnp.concatenate([b_query, b_key, b_value]).astype(f32)[None, :]
    last_args = bias, cosine, sine
    rows = add_up(fars, all_rows[:2], (feature(2, z), feature(2, o)), sums, last_args)

    others = lax.ppermute(rows, "cand", ACROSS_Z_HI)
    near = attention(0, ALL, lists, [rows], kv_parts)
    others = tie(others, near)
    for_other = attention(1, ALL, lists, [others], kv_parts)
    back = lax.ppermute(for_other, "cand", ACROSS_Z_HI)
    attended = jnp.where(traits[:, 1:] > 0.5, near, back)

    cut = width // 2

    def term(d, z, attended, first=0, last=width):
        start = feature(d, z) + first
        return dot(attended, lax.dynamic_slice(w_out, (0, start), (w_out.shape[0], last - first)))

    later, far = attended, []
    for side in (o, z):
        left = term(2, side, later, 0, cut).astype(bf16)
        right = term(2, side, tie(attended, left), cut, width).astype(bf16)
        far.append((pass_up(left), pass_down(right)))
        later = tie(attended, right)
    near_sums = []
    for side, (left, right) in zip((o, z), far):
        later = tie(attended, left, right)
        up, down = term(1, side, later), term(3, side, later)
        up = jnp.concatenate([up[:, :cut] + left.astype(f32), up[:, cut:]], 1).astype(bf16)
        down = jnp.concatenate([down[:, :cut], down[:, cut:] + right.astype(f32)], 1).astype(bf16)
        last = tie(attended, up, down)
        near_sums.append((tie(term(0, side, last), up), pass_up(up), pass_down(down)))
    (own, up, down), rest = near_sums[0], near_sums[1]
    crossed = pass_over((own + up.astype(f32) + down.astype(f32)).astype(bf16))
    return finish(spread, flat, *rest, crossed).reshape(tokens.shape)


def solution(mesh):
    in_specs = (
        P("cand", None, "tp"),
        P(),
        P(None, "tp"),
        P("tp"),
        P(None, "tp"),
        P("tp"),
        P(None, "tp"),
        P("tp"),
        P("tp", None),
        P("cand", None, "tp"),
        P("cand", None, "tp"),
        P(),
        P("cand", None),
        P("cand"),
    )
    out_specs = P("cand", None, "tp")
    return jax.shard_map(
        on_device, mesh=mesh, in_specs=in_specs, out_specs=out_specs, check_vma=False
    )
```
